1024 devices in a mesh: grp: 64 (over x, z), loc: 16 (over y, core).
Axes of the slice: x: 4, y: 8, z: 16, core: 2. Of those that a mesh axis runs over, the one named last changes fastest.
Arguments:
- inputs: bfloat16 [8192, 2048], P('grp', 'loc'), may hold values from -6 to 6
- out_grad: bfloat16 [8192, 2048], P('grp', 'loc'), may hold values from -6 to 6
- expert_ids: int32 [8192, 10], P('grp'), may hold values from 0 to 511, as said below
- gate_probs: bfloat16 [8192, 10], P('grp'), may hold values from 0.049804688 to 0.5
- group_slot: int32 [8192, 10], P('grp'), may hold values from 0 to 24, as said below
- w_gate: bfloat16 [1024, 2048, 256], P(('grp', 'loc')), may hold values from -0.125 to 0.125
- w_up: bfloat16 [1024, 2048, 256], P(('grp', 'loc')), may hold values from -0.125 to 0.125
- w_down: bfloat16 [1024, 256, 2048], P(('grp', 'loc')), may hold values from -0.25 to 0.25
Outputs:
- in_grad: bfloat16 [8192, 2048], P('grp', 'loc')
- gate_grad: bfloat16 [8192, 10], P('grp')
The draws below stay inside these ranges and needn't reach their ends.
Inputs may be any that keep to these rules, and one draw needn't show every extreme that they name: `expert_ids`: each row names 10 different experts. `group_slot`: picks of one token into one group share one value. Among the tokens of one grp index bound to one group, the values below 24 number the first of them 0, 1, 2, ... in token order; 24 means the token is not sent to that group.
All inputs are finite; a program needn't handle non-finite values.
Results may differ from the reference program's by a relative error of at most 0.0065.
Values may be sent and summed in bfloat16 or wider, within the bound.
A program may use at most 32 MiB of HBM per device.

```python
import math
import jax
import jax.numpy as jnp
from jax import lax

D = 2048
FF = 512
TOP = 10
TOK_GRP = 128
SEND = 24
ROOM = 256
EXP_GRP = 8
EXPERTS = 512
TOKENS = 8192
N_GRP = 64


def routing(key):
    pick_key = jax.random.fold_in(key, 101)
    order_key = jax.random.fold_in(key, 202)
    hot_key = jax.random.fold_in(key, 303)
    side_key = jax.random.fold_in(key, 404)
    ranking = jax.random.permutation(order_key, EXPERTS)
    lift = jnp.where(ranking < max(1, EXPERTS // 16), 1966, 0).astype(jnp.int32)
    hot_group = jax.random.randint(hot_key, (), 0, N_GRP, dtype=jnp.int32)
    side = jax.random.randint(side_key, (TOKENS,), 0, EXP_GRP, dtype=jnp.int32)
    forced = hot_group * EXP_GRP + side
    boost = jnp.where(jnp.arange(EXPERTS, dtype=jnp.int32)[None, :] == forced[:, None], 65536, 0).astype(jnp.int32)
    base = jax.random.randint(pick_key, (TOKENS, EXPERTS), 0, 65536, dtype=jnp.int32)
    score = (base + lift[None, :] + boost) * EXPERTS + jnp.arange(EXPERTS, dtype=jnp.int32)[None, :]
    unused, chosen = lax.top_k(score, TOP)
    chosen = chosen.astype(jnp.int32)
    group = chosen // EXP_GRP
    touch = jnp.any(group[:, :, None] == jnp.arange(N_GRP, dtype=jnp.int32)[None, None, :], axis=1).astype(jnp.int32)
    per_block = touch.reshape(-1, TOK_GRP, N_GRP)
    before = (jnp.cumsum(per_block, axis=1) - per_block).reshape(TOKENS, N_GRP)
    gslot = jnp.minimum(jnp.take_along_axis(before, group, axis=1), SEND).astype(jnp.int32)
    return (chosen, gslot)


def draw_expert_ids(key, part):
    return routing(key)[0]


def draw_group_slot(key, part):
    return routing(key)[1]


def level_of(stream_key, shape, shards, low, top_value):
    loudness = 1.0
    for dim, shards_of in shards:
        draws = jax.random.uniform(jax.random.fold_in(jax.random.fold_in(stream_key, 6), dim), (shards_of,), jnp.float32, low / len(shards), top_value / len(shards))
        loudness = loudness * jnp.repeat(jnp.exp(draws), shape[dim] // shards_of).reshape((-1,) + (1,) * (len(shape) - 1 - dim))
    return loudness


def normal_values(key, dims, width, bound, pieces=(), held_as=jnp.bfloat16):
    result = width * jax.random.normal(key, dims, jnp.float32)
    if pieces:
        result = result * level_of(key, dims, pieces, -0.22, 0.18)
    return jnp.clip(result, -bound, bound).astype(held_as)


def setup_inputs(seed: int = 0) -> dict:
    key_of = jax.random.split(jax.random.key(seed), 9)
    inputs = normal_values(key_of[0], (TOKENS, D), 1.0, 6.0, ((0, 64), (1, 16)))
    out_grad = normal_values(key_of[1], (TOKENS, D), 1.0, 6.0, ((0, 64), (1, 16)))
    expert_ids = draw_expert_ids(jax.random.fold_in(key_of[8], 71), 0)
    gate_probs = jnp.clip(jnp.exp(math.log(0.5) - 2.306499 * jax.random.uniform(key_of[3], (TOKENS, TOP), jnp.float32) ** level_of(key_of[3], (TOKENS, TOP), ((0, 64),), -0.2, 0.2)), 0.049804688, 0.5).astype(jnp.bfloat16)
    group_slot = draw_group_slot(jax.random.fold_in(key_of[8], 71), 0)
    w_gate = normal_values(key_of[5], (2 * EXPERTS, D, FF // 2), D ** -0.5, 0.125, ((0, 1024),))
    w_up = normal_values(key_of[6], (2 * EXPERTS, D, FF // 2), D ** -0.5, 0.125, ((0, 1024),))
    w_down = normal_values(key_of[7], (2 * EXPERTS, FF // 2, D), FF ** -0.5, 0.25, ((0, 1024),))
    return dict(inputs=inputs, out_grad=out_grad, expert_ids=expert_ids, gate_probs=gate_probs, group_slot=group_slot, w_gate=w_gate, w_up=w_up, w_down=w_down)


def expert_half(rows_x, rows_dy, rows_gate, wg, wu, wd):
    gate_pre = jnp.dot(rows_x, wg, preferred_element_type=jnp.float32)
    up_pre = jnp.dot(rows_x, wu, preferred_element_type=jnp.float32)
    sig = jax.nn.sigmoid(gate_pre)
    act = gate_pre * sig
    back = lax.dot_general(rows_dy, wd, (((1,), (1,)), ((), ())), preferred_element_type=jnp.float32)
    scaled = rows_gate.astype(jnp.float32)[:, None] * back
    gate_diff = (scaled * up_pre * (sig * (1.0 + gate_pre * (1.0 - sig)))).astype(jnp.bfloat16)
    up_diff = (scaled * act).astype(jnp.bfloat16)
    in_part = lax.dot_general(gate_diff, wg, (((1,), (1,)), ((), ())), preferred_element_type=jnp.float32)
    in_part = in_part + lax.dot_general(up_diff, wu, (((1,), (1,)), ((), ())), preferred_element_type=jnp.float32)
    weight_part = jnp.sum(act * up_pre * back, axis=1)
    return in_part.astype(jnp.bfloat16), weight_part.astype(jnp.bfloat16)


def reference(inputs, out_grad, expert_ids, gate_probs, group_slot, w_gate, w_up, w_down):
    count = ROOM
    picks = TOKENS * TOP
    sent = group_slot < SEND
    token_ids = jnp.broadcast_to(jnp.arange(TOKENS, dtype=jnp.int32)[:, None], (TOKENS, TOP))
    counts = jnp.zeros((TOKENS, EXPERTS), jnp.int32).at[token_ids, expert_ids].add(sent.astype(jnp.int32))
    before = (jnp.cumsum(counts, axis=0) - counts).astype(jnp.int32)
    rank = jnp.take_along_axis(before, expert_ids, axis=1).astype(jnp.int32)
    live = sent & (rank < ROOM)
    column = jnp.where(live, rank, count).reshape(-1).astype(jnp.int32)
    table = jnp.full((EXPERTS, count), picks, jnp.int32)
    table = table.at[expert_ids.reshape(-1), column].set(jnp.arange(picks, dtype=jnp.int32), mode="drop")
    flat_gate = gate_probs.reshape(-1)

    def one_expert(carry, expert):
        group_sum, gate_out = carry
        rows = table[expert]
        valid = rows < picks
        token = jnp.where(valid, rows // TOP, 0).astype(jnp.int32)
        rows_x = jnp.where(valid[:, None], inputs[token], jnp.zeros((), inputs.dtype))
        rows_dy = jnp.where(valid[:, None], out_grad[token], jnp.zeros((), out_grad.dtype))
        rows_gate = jnp.where(valid, flat_gate[jnp.minimum(rows, picks - 1)], jnp.zeros((), flat_gate.dtype))
        total_x = jnp.zeros((count, D), jnp.float32)
        total_g = jnp.zeros((count,), jnp.float32)
        for half in range(2):
            index = 2 * expert + half
            in_part, weight_part = expert_half(rows_x, rows_dy, rows_gate, w_gate[index], w_up[index], w_down[index])
            in_part, weight_part = lax.optimization_barrier((in_part, weight_part))
            total_x = total_x + in_part.astype(jnp.float32)
            total_g = total_g + weight_part.astype(jnp.float32)
        target = jnp.where(valid, token, TOKENS).astype(jnp.int32)
        group_sum = group_sum.at[target].add(total_x, mode="drop")
        slot_target = jnp.where(valid, rows, picks).astype(jnp.int32)
        gate_out = gate_out.at[slot_target].set(total_g.astype(gate_out.dtype), mode="drop")
        return (group_sum, gate_out), None

    def one_group(carry, group):
        total, gate_out = carry
        members = (group * EXP_GRP + jnp.arange(EXP_GRP, dtype=jnp.int32)).astype(jnp.int32)
        start = (jnp.zeros((TOKENS, D), jnp.float32), gate_out)
        (group_sum, gate_out), _ = lax.scan(one_expert, start, members)
        rounded = lax.optimization_barrier(group_sum.astype(jnp.bfloat16))
        total = total + rounded.astype(jnp.float32)
        return (total, gate_out), None

    start = (jnp.zeros((TOKENS, D), jnp.float32), jnp.zeros((picks,), jnp.bfloat16))
    (total, gate_out), _ = lax.scan(one_group, start, jnp.arange(N_GRP, dtype=jnp.int32))
    return total.astype(jnp.bfloat16), gate_out.reshape(TOKENS, TOP)
```

```python
import jax
import jax.numpy as jnp
from jax import lax
from jax.sharding import PartitionSpec as P

F32 = jnp.float32
BF16 = jnp.bfloat16
I32 = jnp.int32


def dot(a, b):
    return jnp.dot(a, b, preferred_element_type=F32)


def expert_half(rows_x, rows_dy, rows_gate, wg, wu, wd):
    g = dot(rows_x, wg)
    u = dot(rows_x, wu)
    b = lax.dot_general(rows_dy, wd, (((1,), (1,)), ((), ())), preferred_element_type=F32)
    s = jax.nn.sigmoid(g)
    a = g * s
    q = rows_gate.astype(F32)[:, None] * b
    dg = (q * u * (s * (1.0 + g * (1.0 - s)))).astype(BF16)
    du = (q * a).astype(BF16)
    part = lax.dot_general(dg, wg, (((1,), (1,)), ((), ())), preferred_element_type=F32)
    part = part + lax.dot_general(du, wu, (((1,), (1,)), ((), ())), preferred_element_type=F32)
    return part, jnp.sum(a * u * b, axis=1)


def shards(inputs, out_grad, expert_ids, gate_probs, group_slot, w_gate, w_up, w_down):
    n_grp = lax.axis_size("grp")
    n_loc = lax.axis_size("loc")
    exp_grp = n_loc // 2
    tok, wide = inputs.shape
    room = 2 * tok
    send = max(1, 3 * tok // 16)
    lanes = n_grp * send
    meta = 256
    pad = meta // exp_grp
    c_rows = room // wide
    core = lax.axis_index("loc") % 2
    mine = lax.axis_index("loc") // 2

    group = expert_ids // exp_grp
    member = expert_ids % exp_grp
    sent = group_slot < send
    lane = jnp.where(sent, group * send + group_slot, lanes)
    place = jnp.any(
        lane.T[None] == jnp.arange(lanes, dtype=I32)[:, None, None], axis=1
    ).astype(BF16)
    field = jnp.where(sent, member * pad + group_slot, meta).reshape(-1)
    of_group = (group.reshape(-1)[None, :] == jnp.arange(n_grp, dtype=I32)[:, None]).astype(BF16)
    of_field = field[:, None] == jnp.arange(meta, dtype=I32)[None, :]
    marks = dot(
        of_group, jnp.where(of_field, gate_probs.reshape(-1)[:, None], jnp.zeros((), BF16))
    ).astype(BF16)
    both = jnp.concatenate([inputs, out_grad], 1)
    packed = dot(place, both).astype(BF16).reshape(n_grp, send, 2 * wide)
    outgoing = jnp.concatenate(
        [packed[:, :, :wide], packed[:, :, wide:], marks.reshape(n_grp, meta // wide, wide)], 1
    )
    got = lax.all_to_all(outgoing, "grp", split_axis=0, concat_axis=0, tiled=True)

    rows = jnp.concatenate([got[:, :send], got[:, send : 2 * send]], 2).reshape(lanes, 2 * wide)
    got_marks = got[:, 2 * send :].reshape(n_grp, meta)
    picked = got_marks != 0
    count = picked.astype(BF16)
    f_row = jnp.arange(meta, dtype=I32)[:, None]
    f_col = jnp.arange(meta, dtype=I32)[None, :]
    same = f_row // pad == f_col // pad
    within = dot(count, (same & (f_row <= f_col)).astype(BF16))
    total = dot(count, same.astype(BF16)).astype(BF16)
    earlier = (
        jnp.arange(n_grp, dtype=I32)[None, :] < jnp.arange(n_grp, dtype=I32)[:, None]
    ).astype(BF16)
    rank = within + dot(earlier, total) - 1.0
    rank = jnp.where(picked & (rank < room), rank, 2.0 * room).astype(I32)
    by_lane = rank.reshape(n_grp, exp_grp, pad)[:, :, :send].transpose(1, 0, 2).reshape(exp_grp, lanes)
    gate_lane = (
        got_marks.reshape(n_grp, exp_grp, pad)[:, :, :send].transpose(1, 0, 2).reshape(exp_grp, lanes)
    )
    pick_of = (by_lane[:, None, :] == jnp.arange(room, dtype=I32)[None, :, None]).astype(BF16)
    fan = dot(pick_of.reshape(exp_grp * room, lanes), rows).astype(BF16)
    fan = fan.reshape(exp_grp, room, 2 * wide)
    my_rank = lax.dynamic_index_in_dim(by_lane, mine, 0, keepdims=False)
    my_gate = lax.dynamic_index_in_dim(gate_lane, mine, 0, keepdims=False)
    my_pick = my_rank[None, :] == jnp.arange(room, dtype=I32)[:, None]
    gates = jnp.sum(jnp.where(my_pick, my_gate.astype(F32)[None, :], 0.0), axis=1)

    same_core = [[2 * y + c for y in range(exp_grp)] for c in range(2)]
    swap = [(i, i ^ 1) for i in range(n_loc)]
    own = lax.all_to_all(
        fan, "loc", split_axis=0, concat_axis=0, axis_index_groups=same_core, tiled=True
    )
    other = lax.ppermute(own, "loc", swap)
    low = jnp.where(core == 0, own, other)
    high = jnp.where(core == 0, other, own)
    full = jnp.stack([low, high], 1).reshape(n_loc, room, 2, wide).transpose(2, 1, 0, 3)
    full = full.reshape(2, room, n_loc * wide)
    part, c_part = expert_half(full[0], full[1], gates, w_gate[0], w_up[0], w_down[0])

    blocks = part.reshape(room, exp_grp, 2, wide).transpose(2, 1, 0, 3)
    keep = jnp.where(core == 0, blocks[0], blocks[1])
    give = jnp.where(core == 0, blocks[1], blocks[0]).astype(BF16)
    given = lax.ppermute(give, "loc", swap).astype(F32)
    c_given = lax.ppermute(c_part.astype(BF16), "loc", swap).astype(F32)
    pair_x = (keep + given).astype(BF16)
    pair_c = (c_part.astype(BF16).astype(F32) + c_given).astype(BF16)
    pair_c = jnp.broadcast_to(pair_c.reshape(1, c_rows, wide), (exp_grp, c_rows, wide))
    back = lax.all_to_all(
        jnp.concatenate([pair_x, pair_c], 1),
        "loc",
        split_axis=0,
        concat_axis=0,
        axis_index_groups=same_core,
        tiled=True,
    )
    slot_x = back[:, :room].reshape(exp_grp * room, wide)
    slot_c = back[:, room:].reshape(exp_grp, room)
    summed = lax.dot_general(
        pick_of.reshape(exp_grp * room, lanes),
        slot_x,
        (((0,), (0,)), ((), ())),
        preferred_element_type=F32,
    ).astype(BF16)
    lane_c = jnp.einsum("mr,mrl->ml", slot_c, pick_of, preferred_element_type=F32).astype(BF16)
    home_c = jnp.pad(
        lane_c.reshape(exp_grp, n_grp, send).transpose(1, 0, 2), ((0, 0), (0, 0), (0, pad - send))
    ).reshape(n_grp, meta // wide, wide)
    home = lax.all_to_all(
        jnp.concatenate([summed.reshape(n_grp, send, wide), home_c], 1),
        "grp",
        split_axis=0,
        concat_axis=0,
        tiled=True,
    )
    in_grad = lax.dot_general(
        place,
        home[:, :send].reshape(lanes, wide),
        (((0,), (0,)), ((), ())),
        preferred_element_type=F32,
    ).astype(BF16)
    table = home[:, send:].reshape(n_grp, meta)
    picks = lax.dot_general(
        of_group, table, (((0,), (0,)), ((), ())), preferred_element_type=F32
    )
    gate_grad = jnp.sum(jnp.where(of_field, picks, 0.0), axis=1).astype(BF16)
    return in_grad, gate_grad.reshape(expert_ids.shape)


def solution(mesh):
    return jax.shard_map(
        shards,
        mesh=mesh,
        in_specs=(
            P("grp", "loc"),
            P("grp", "loc"),
            P("grp", None),
            P("grp", None),
            P("grp", None),
            P(("grp", "loc"), None, None),
            P(("grp", "loc"), None, None),
            P(("grp", "loc"), None, None),
        ),
        out_specs=(P("grp", "loc"), P("grp", None)),
        check_vma=False,
    )
```

```python
import jax
import jax.numpy as jnp
from jax import lax
from jax.experimental import pallas as pl
from jax.experimental.pallas import tpu as pltpu
from jax.sharding import PartitionSpec as P

MESH = pl.DeviceIdType.MESH

F32 = jnp.float32
BF16 = jnp.bfloat16
I32 = jnp.int32


def dot(a, b):
    return jnp.dot(a, b, preferred_element_type=F32)


def ring_offset(i, n):
    half = (i + 1) // 2
    return n // 2 + jnp.where(i % 2 == 0, half, -half)


def middle_kernel(
    rows_ref, rank_row, rank_col, gate_ref, wg_ref, wu_ref, wd_ref,
    out_x, out_c,
    fan_x, fan_dy, full_x, full_dy, acc_g, acc_u, acc_b, dg_ref, du_ref,
    keep, give, got, pair, back, c_own, c_got, c_all, acc,
    fan_ss, fan_rs, twin_ss, twin_rs, give_ss, give_rs, ret_ss, ret_rs,
    cx_ss, cx_rs, cr_ss, cr_rs,
):
    n = full_x.shape[0]
    room, wide = fan_x.shape[1:]
    lanes = rows_ref.shape[0]
    grp = lax.axis_index("grp")
    loc = lax.axis_index("loc")
    y, core = loc // 2, loc % 2
    twin = (grp, 2 * y + 1 - core)
    my_cols = pl.ds(pl.multiple_of(core * wide, wide), wide)

    def peer(yy):
        return (grp, 2 * yy + core)

    def rdma(src, dst, ss, rs, to):
        return pltpu.make_async_remote_copy(
            src_ref=src, dst_ref=dst, send_sem=ss, recv_sem=rs, device_id=to, device_id_type=MESH
        )

    def fan_copy(m, slot, k):
        src, dst = ((fan_dy, full_dy), (fan_x, full_x))[k]
        return rdma(
            src.at[m], dst.at[slot, :, my_cols], fan_ss.at[m, k], fan_rs.at[slot, k], peer(m)
        )

    def twin_copy(slot, k):
        buf = (full_dy, full_x)[k]
        return rdma(
            buf.at[slot, :, my_cols], buf.at[slot, :, my_cols],
            twin_ss.at[slot, k], twin_rs.at[slot, k], twin,
        )

    def twin_arrival(slot, k):
        buf = (full_dy, full_x)[k]
        cols = pl.ds(pl.multiple_of((1 - core) * wide, wide), wide)
        return rdma(
            buf.at[slot, :, cols], buf.at[slot, :, cols],
            twin_ss.at[slot, k], twin_rs.at[slot, k], twin,
        )

    barrier = pltpu.get_barrier_semaphore()

    def greet(i, _):
        pl.semaphore_signal(barrier, inc=1, device_id=peer((y + i) % n), device_id_type=MESH)
        return _

    lax.fori_loop(1, n, greet, 0)
    pl.semaphore_signal(barrier, inc=1, device_id=twin, device_id_type=MESH)
    pl.semaphore_wait(barrier, n)

    slot_iota = lax.broadcasted_iota(I32, (room, lanes), 0).astype(F32)

    def spread(i, _):
        m = (y + ring_offset(i, n)) % n
        pick = (rank_row[m] == slot_iota).astype(F32).astype(BF16)
        block = dot(pick, rows_ref[...]).astype(BF16)

        @pl.when(i < n - 1)
        def _far():
            fan_x[m] = block[:, :wide]
            fan_dy[m] = block[:, wide:]
            fan_copy(m, y, 0).start()
            fan_copy(m, y, 1).start()

        @pl.when(i == n - 1)
        def _near():
            full_x[y, :, my_cols] = block[:, :wide]
            full_dy[y, :, my_cols] = block[:, wide:]
            twin_copy(y, 0).start()
            twin_copy(y, 1).start()

        return _

    lax.fori_loop(0, n, spread, 0)

    acc_g[...] = jnp.zeros_like(acc_g)
    acc_u[...] = jnp.zeros_like(acc_u)
    acc_b[...] = jnp.zeros_like(acc_b)

    def source(i):
        return (y + n - ring_offset(i, n)) % n

    def multiply(slot):
        twin_arrival(slot, 0).wait_recv()
        twin_arrival(slot, 1).wait_recv()
        rows = pl.ds(pl.multiple_of(slot * 2 * wide, 2 * wide), 2 * wide)
        xs = full_x[slot]
        acc_b[...] += lax.dot_general(
            full_dy[slot], wd_ref[:, rows], (((1,), (1,)), ((), ())), preferred_element_type=F32
        )
        acc_g[...] += dot(xs, wg_ref[rows, :])
        acc_u[...] += dot(xs, wu_ref[rows, :])

    def gather(i, _):
        slot = source(i)
        fan_copy(slot, slot, 0).wait_recv()
        twin_copy(slot, 0).start()
        fan_copy(slot, slot, 1).wait_recv()
        twin_copy(slot, 1).start()
        multiply(jnp.where(i == 0, y, source(jnp.maximum(i - 1, 0))))
        return _

    lax.fori_loop(0, n - 1, gather, 0)
    multiply(source(n - 2))

    g = acc_g[...]
    u = acc_u[...]
    b = acc_b[...]
    s = 1.0 / (1.0 + jnp.exp(-g))
    a = g * s
    q = gate_ref[...] * b
    dg_ref[...] = (q * u * (s * (1.0 + g * (1.0 - s)))).astype(BF16)
    du_ref[...] = (q * a).astype(BF16)
    gate_part = a * u * b
    high = gate_part.astype(BF16)
    low = (gate_part - high.astype(F32)).astype(BF16)
    ones = jnp.ones((8, gate_part.shape[1]), BF16)
    nt = (((1,), (1,)), ((), ()))
    c_half = lax.dot_general(ones, high, nt, preferred_element_type=F32) + lax.dot_general(
        ones, low, nt, preferred_element_type=F32
    )
    c_own[...] = c_half.astype(BF16).astype(F32)
    rdma(c_own, c_got, cx_ss, cx_rs, twin).start()

    def give_copy(t):
        return rdma(give.at[t], got.at[t], give_ss.at[t], give_rs.at[t], twin)

    def ret_copy(t, slot):
        return rdma(pair.at[t], back.at[slot], ret_ss.at[t], ret_rs.at[slot], peer(t))

    def c_copy(t, slot):
        return rdma(c_all.at[y], c_all.at[slot], cr_ss.at[t], cr_rs.at[slot], peer(t))

    def target(i):
        return (y + ring_offset(i, n)) % n

    def add_pair(i):
        t = target(i)
        give_copy(t).wait_recv()
        total = (keep[t] + got[t].astype(F32)).astype(BF16)

        @pl.when(i < n - 1)
        def _far():
            pair[t] = total
            ret_copy(t, y).start()

        @pl.when(i == n - 1)
        def _near():
            back[y] = total

    def produce(i, _):
        t = target(i)
        rows = pl.ds(pl.multiple_of(t * 2 * wide, 2 * wide), 2 * wide)
        part = lax.dot_general(dg_ref[...], wg_ref[rows, :], nt, preferred_element_type=F32)
        part = part + lax.dot_general(du_ref[...], wu_ref[rows, :], nt, preferred_element_type=F32)
        left, right = part[:, :wide], part[:, wide:]
        keep[t] = jnp.where(core == 0, left, right)
        give[t] = jnp.where(core == 0, right, left).astype(BF16)
        give_copy(t).start()

        @pl.when(i > 0)
        def _before():
            add_pair(jnp.maximum(i - 1, 0))

        return _

    lax.fori_loop(0, n, produce, 0)
    add_pair(n - 1)

    rdma(c_own, c_got, cx_ss, cx_rs, twin).wait_recv()
    c_all[y] = (c_own[...] + c_got[...]).astype(BF16).astype(F32)

    def c_send(i, _):
        c_copy(target(i), y).start()
        return _

    lax.fori_loop(0, n - 1, c_send, 0)

    acc[...] = jnp.zeros_like(acc)
    lane_iota = lax.broadcasted_iota(I32, (lanes, room), 1).astype(F32)
    eye = lax.broadcasted_iota(I32, (room, room), 0) == lax.broadcasted_iota(I32, (room, room), 1)
    col_iota = lax.broadcasted_iota(I32, (room, wide), 1)
    pick_row = lax.broadcasted_iota(I32, (wide, room), 0)

    def combine(slot):
        rank = dot(rank_col[...], (pick_row == slot).astype(F32).astype(BF16))
        pick = (rank == lane_iota).astype(F32).astype(BF16)
        c_col = jnp.sum(jnp.where(eye, c_all[slot][:1, :], 0.0), axis=1, keepdims=True)
        c_cols = jnp.where(col_iota == slot, c_col, 0.0).astype(BF16)
        acc[...] += dot(pick, jnp.concatenate([back[slot], c_cols], axis=1))

    combine(y)

    def collect(i, _):
        slot = source(i)
        ret_copy(slot, slot).wait_recv()
        c_copy(slot, slot).wait_recv()
        combine(slot)
        return _

    lax.fori_loop(0, n - 1, collect, 0)
    out_x[...] = acc[:, :wide].astype(BF16)
    out_c[...] = acc[:, wide:].astype(BF16)

    def drain(i, _):
        t = target(i)
        fan_copy(t, y, 0).wait_send()
        fan_copy(t, y, 1).wait_send()
        ret_copy(t, y).wait_send()
        c_copy(t, y).wait_send()
        return _

    lax.fori_loop(0, n - 1, drain, 0)

    def drain_twin(i, _):
        twin_copy(i, 0).wait_send()
        twin_copy(i, 1).wait_send()
        give_copy(i).wait_send()
        return _

    lax.fori_loop(0, n, drain_twin, 0)
    rdma(c_own, c_got, cx_ss, cx_rs, twin).wait_send()


def middle(rows, rank_row, rank_col, gates, wg, wu, wd):
    lanes = rows.shape[0]
    n, room, wide = rank_row.shape[0], gates.shape[0], rows.shape[1] // 2
    hidden = wg.shape[1]
    dma = pltpu.SemaphoreType.DMA
    block = (n, room, wide)
    vmem = pl.BlockSpec(memory_space=pltpu.VMEM)
    return pl.pallas_call(
        middle_kernel,
        out_shape=(
            jax.ShapeDtypeStruct((lanes, wide), BF16),
            jax.ShapeDtypeStruct((lanes, wide), BF16),
        ),
        in_specs=[vmem] * 7,
        out_specs=(vmem, vmem),
        scratch_shapes=[
            pltpu.VMEM(block, BF16),
            pltpu.VMEM(block, BF16),
            pltpu.VMEM((n, room, 2 * wide), BF16),
            pltpu.VMEM((n, room, 2 * wide), BF16),
            pltpu.VMEM((room, hidden), F32),
            pltpu.VMEM((room, hidden), F32),
            pltpu.VMEM((room, hidden), F32),
            pltpu.VMEM((room, hidden), BF16),
            pltpu.VMEM((room, hidden), BF16),
            pltpu.VMEM(block, F32),
            pltpu.VMEM(block, BF16),
            pltpu.VMEM(block, BF16),
            pltpu.VMEM(block, BF16),
            pltpu.VMEM(block, BF16),
            pltpu.VMEM((8, room), F32),
            pltpu.VMEM((8, room), F32),
            pltpu.VMEM((n, 8, room), F32),
            pltpu.VMEM((lanes, 2 * wide), F32),
            dma((n, 2)),
            dma((n, 2)),
            dma((n, 2)),
            dma((n, 2)),
            dma((n,)),
            dma((n,)),
            dma((n,)),
            dma((n,)),
            dma,
            dma,
            dma((n,)),
            dma((n,)),
        ],
        compiler_params=pltpu.CompilerParams(
            collective_id=0, has_side_effects=True, vmem_limit_bytes=40 << 20
        ),
        cost_estimate=pl.CostEstimate(
            flops=10 * room * hidden * n * 2 * wide, bytes_accessed=8 << 20, transcendentals=0
        ),
    )(rows, rank_row, rank_col, gates, wg, wu, wd)


def shards(inputs, out_grad, expert_ids, gate_probs, group_slot, w_gate, w_up, w_down):
    n_grp = lax.axis_size("grp")
    n_loc = lax.axis_size("loc")
    exp_grp = n_loc // 2
    tok, wide = inputs.shape
    room = 2 * tok
    send = max(1, 3 * tok // 16)
    lanes = n_grp * send
    meta = 256
    pad = meta // exp_grp
    mine = lax.axis_index("loc") // 2

    group = expert_ids // exp_grp
    member = expert_ids % exp_grp
    sent = group_slot < send
    lane = jnp.where(sent, group * send + group_slot, lanes)
    place = jnp.any(
        lane.T[None] == jnp.arange(lanes, dtype=I32)[:, None, None], axis=1
    ).astype(BF16)
    field = jnp.where(sent, member * pad + group_slot, meta).reshape(-1)
    of_group = (group.reshape(-1)[None, :] == jnp.arange(n_grp, dtype=I32)[:, None]).astype(BF16)
    of_field = field[:, None] == jnp.arange(meta, dtype=I32)[None, :]
    marks = dot(
        of_group, jnp.where(of_field, gate_probs.reshape(-1)[:, None], jnp.zeros((), BF16))
    ).astype(BF16)
    both = jnp.concatenate([inputs, out_grad], 1)
    packed = dot(place, both).astype(BF16).reshape(n_grp, send, 2 * wide)
    outgoing = jnp.concatenate(
        [packed[:, :, :wide], packed[:, :, wide:], marks.reshape(n_grp, meta // wide, wide)], 1
    )
    got = lax.all_to_all(outgoing, "grp", split_axis=0, concat_axis=0, tiled=True)

    rows = jnp.concatenate([got[:, :send], got[:, send : 2 * send]], 2).reshape(lanes, 2 * wide)
    got_marks = got[:, 2 * send :].reshape(n_grp, meta)
    picked = got_marks != 0
    count = picked.astype(BF16)
    f_row = jnp.arange(meta, dtype=I32)[:, None]
    f_col = jnp.arange(meta, dtype=I32)[None, :]
    same = f_row // pad == f_col // pad
    within = dot(count, (same & (f_row <= f_col)).astype(BF16))
    total = dot(count, same.astype(BF16)).astype(BF16)
    earlier = (
        jnp.arange(n_grp, dtype=I32)[None, :] < jnp.arange(n_grp, dtype=I32)[:, None]
    ).astype(BF16)
    rank = within + dot(earlier, total) - 1.0
    rank = jnp.where(picked & (rank < room), rank, 2.0 * room).astype(I32)
    by_lane = rank.reshape(n_grp, exp_grp, pad)[:, :, :send].transpose(1, 0, 2).reshape(exp_grp, lanes)
    gate_lane = (
        got_marks.reshape(n_grp, exp_grp, pad)[:, :, :send].transpose(1, 0, 2).reshape(exp_grp, lanes)
    )
    my_rank = lax.dynamic_index_in_dim(by_lane, mine, 0, keepdims=False)
    my_gate = lax.dynamic_index_in_dim(gate_lane, mine, 0, keepdims=False)
    my_pick = my_rank[None, :] == jnp.arange(room, dtype=I32)[:, None]
    gates = jnp.sum(jnp.where(my_pick, my_gate.astype(F32)[None, :], 0.0), axis=1, keepdims=True)
    summed, lane_c = middle(
        rows,
        by_lane.astype(F32).reshape(exp_grp, 1, lanes),
        jnp.pad(by_lane.astype(BF16).T, ((0, 0), (0, wide - exp_grp))),
        gates,
        w_gate[0],
        w_up[0],
        w_down[0],
    )
    lane_c = lane_c[:, :exp_grp].T
    home_c = jnp.pad(
        lane_c.reshape(exp_grp, n_grp, send).transpose(1, 0, 2), ((0, 0), (0, 0), (0, pad - send))
    ).reshape(n_grp, meta // wide, wide)
    home = lax.all_to_all(
        jnp.concatenate([summed.reshape(n_grp, send, wide), home_c], 1),
        "grp",
        split_axis=0,
        concat_axis=0,
        tiled=True,
    )
    in_grad = lax.dot_general(
        place,
        home[:, :send].reshape(lanes, wide),
        (((0,), (0,)), ((), ())),
        preferred_element_type=F32,
    ).astype(BF16)
    table = home[:, send:].reshape(n_grp, meta)
    picks = lax.dot_general(
        of_group, table, (((0,), (0,)), ((), ())), preferred_element_type=F32
    )
    gate_grad = jnp.sum(jnp.where(of_field, picks, 0.0), axis=1).astype(BF16)
    return in_grad, gate_grad.reshape(expert_ids.shape)


def solution(mesh):
    return jax.shard_map(
        shards,
        mesh=mesh,
        in_specs=(
            P("grp", "loc"),
            P("grp", "loc"),
            P("grp", None),
            P("grp", None),
            P("grp", None),
            P(("grp", "loc"), None, None),
            P(("grp", "loc"), None, None),
            P(("grp", "loc"), None, None),
        ),
        out_specs=(P("grp", "loc"), P("grp", None)),
        check_vma=False,
    )
```

```python
import jax
import jax.numpy as jnp
from jax import lax
from jax.experimental import pallas as pl
from jax.experimental.pallas import tpu as pltpu
from jax.sharding import PartitionSpec as P

MESH = pl.DeviceIdType.MESH
F32 = jnp.float32
BF16 = jnp.bfloat16
I32 = jnp.int32
NX = 4
META = 256
NT = (((1,), (1,)), ((), ()))


def dot(a, b):
    return jnp.dot(a, b, preferred_element_type=F32)


def bits(mask):
    return mask.astype(F32).astype(BF16)


def ring_offset(i, n):
    half = (i + 1) // 2
    return n // 2 + jnp.where(i % 2 == 0, half, -half)


def near_offset(i, n):
    half = (i + 1) // 2
    return jnp.where(i % 2 == 0, n - half, half) % n


def kernel(
    sx_ref, sdy_ref, marks_ref, wg_hbm, wu_hbm, wd_hbm,
    out_x, out_c,
    wg_ref, wu_ref, wd_ref,
    z_dy, z_x, z_marks, x_dy, x_x, l_dy, l_x, l_marks, pick_ref, rank_ref,
    fan_x, fan_dy, full_x, full_dy, acc_g, acc_u, acc_b, dg_ref, du_ref,
    keep, give, got, pair, back, c_own, c_got, c_all, acc,
    o_x, m_x, h_x, o_c, m_c, s_c, h_c, zo_x,
    w_sem, z_ss, z_rs, x_ss, x_rs, xm_ss, xm_rs,
    fan_ss, fan_rs, twin_ss, twin_rs, give_ss, give_rs, ret_ss, ret_rs,
    cx_ss, cx_rs, cr_ss, cr_rs, hx_ss, hx_rs, hc_ss, hc_rs, hz_ss, hz_rs,
):
    n = full_x.shape[0]
    room, wide = fan_x.shape[1:]
    nz, chunk = z_x.shape[:2]
    send = chunk // NX
    two = 2 * send
    pairs = nz // 2
    lanes = nz * chunk
    n_grp = NX * nz
    pad = META // n
    half = META // 2
    grp = lax.axis_index("grp")
    loc = lax.axis_index("loc")
    x, z = grp // nz, grp % nz
    y, core = loc // 2, loc % 2
    twin = (grp, 2 * y + 1 - core)
    my_cols = pl.ds(pl.multiple_of(core * wide, wide), wide)
    twin_cols = pl.ds(pl.multiple_of((1 - core) * wide, wide), wide)

    def rdma(src, dst, ss, rs, to):
        return pltpu.make_async_remote_copy(
            src_ref=src, dst_ref=dst, send_sem=ss, recv_sem=rs, device_id=to, device_id_type=MESH
        )

    def at_z(zz):
        return (x * nz + zz, loc)

    def at_x(xx):
        return (xx * nz + z, loc)

    def peer(yy):
        return (grp, 2 * yy + core)

    loads = [
        pltpu.make_async_copy(src, dst, w_sem.at[i])
        for i, (src, dst) in enumerate(((wg_hbm, wg_ref), (wu_hbm, wu_ref), (wd_hbm, wd_ref)))
    ]
    for load in loads:
        load.start()

    barrier = pltpu.get_barrier_semaphore()

    def greet(to):
        pl.semaphore_signal(barrier, inc=1, device_id=to, device_id_type=MESH)

    def greet_z(i, _):
        greet(at_z((z + i) % nz))
        return _

    def greet_y(i, _):
        greet(peer((y + i) % n))
        return _

    lax.fori_loop(1, nz, greet_z, 0)
    for dx in range(1, NX):
        greet(at_x((x + dx) % NX))
    lax.fori_loop(1, n, greet_y, 0)
    greet(twin)
    pl.semaphore_wait(barrier, nz - 1 + NX - 1 + n - 1 + 1)

    def eight(slot):
        return pl.ds(pl.multiple_of(slot * 8, 8), 8)

    def z_copy(k, to, slot):
        src = (marks_ref, sdy_ref, sx_ref)[k].at[to]
        dst = (z_marks.at[eight(slot)], z_dy.at[slot], z_x.at[slot])[k]
        return rdma(src, dst, z_ss.at[k, to], z_rs.at[k, slot], at_z(to))

    for k in range(3):

        def z_send(i, _, k=k):
            z_copy(k, (z + ring_offset(i, nz)) % nz, z).start()
            return _

        lax.fori_loop(0, nz - 1, z_send, 0)

    z_marks[eight(z)] = marks_ref[z]
    z_dy[z] = sdy_ref[z]
    z_x[z] = sx_ref[z]

    def all_z(slot):
        return pl.ds(pl.multiple_of(slot * nz * 8, 8), nz * 8)

    def marks_copy(to, slot):
        return rdma(z_marks, l_marks.at[all_z(slot)], xm_ss.at[to], xm_rs.at[slot], at_x(to))

    def marks_in(i, _):
        z_copy(0, (z + i) % nz, (z + i) % nz).wait_recv()
        return _

    lax.fori_loop(1, nz, marks_in, 0)
    for dx in range(1, NX):
        marks_copy((x + dx) % NX, x).start()
    l_marks[all_z(x)] = z_marks[...]

    def pair_rows(j):
        return pl.ds(pl.multiple_of(j * two, 16 if two % 16 == 0 else 1), two)

    def x_copy(k, to, slot, j):
        src, dst = ((x_dy, l_dy), (x_x, l_x))[k]
        rows = pair_rows(j)
        return rdma(
            src.at[to, rows], dst.at[slot, rows], x_ss.at[k, to, j], x_rs.at[k, slot, j], at_x(to)
        )

    def onward(k, i):
        src, out, land = ((z_dy, x_dy, l_dy), (z_x, x_x, l_x))[k]
        j = (z // 2 + near_offset(i, pairs)) % pairs
        for zz in range(2):
            slot = 2 * j + zz

            @pl.when(slot != z)
            def _arrival():
                z_copy(1 + k, slot, slot).wait_recv()

        even = src[2 * j].astype(F32)
        odd = src[2 * j + 1].astype(F32)
        rows = pair_rows(j)
        for xx in range(NX):
            part = slice(xx * send, (xx + 1) * send)
            both = jnp.concatenate([even[part], odd[part]], axis=0).astype(BF16)

            @pl.when(xx != x)
            def _far():
                out[xx, rows] = both
                x_copy(k, xx, x, j).start()

            @pl.when(xx == x)
            def _near():
                land[xx, rows] = both

    def onward_dy(i, _):
        onward(0, i)
        return _

    lax.fori_loop(0, pairs, onward_dy, 0)

    for dx in range(1, NX):
        marks_copy((x + dx) % NX, (x + dx) % NX).wait_recv()
    f_row = lax.broadcasted_iota(I32, (half, half), 0)
    f_col = lax.broadcasted_iota(I32, (half, half), 1)
    same = f_row // pad == f_col // pad
    upto = bits(same & (f_row <= f_col))
    block = bits(same)
    earlier = bits(
        lax.broadcasted_iota(I32, (n_grp, n_grp), 1) < lax.broadcasted_iota(I32, (n_grp, n_grp), 0)
    )
    lane_of = lax.broadcasted_iota(I32, (lanes, n_grp), 0)
    src_of = lax.broadcasted_iota(I32, (lanes, n_grp), 1) * send
    from_src = bits((lane_of >= src_of) & (lane_of < src_of + send))
    lane_f = lax.broadcasted_iota(I32, (lanes, half), 0)
    col_f = lax.broadcasted_iota(I32, (lanes, half), 1)
    slot_of = (col_f % pad) == (lane_f % send)
    rank_cols = jnp.zeros((lanes, wide), F32)
    gate_cols = jnp.zeros((lanes, wide), F32)
    per = half // pad
    for ab in range(2):
        marks = l_marks[pl.ds(2 * x + ab, n_grp, 8), :]
        picked = marks != 0.0
        count = bits(picked)
        within = dot(count, upto)
        before = dot(earlier, dot(count, block).astype(BF16))
        rank = within + before - 1.0
        rank = jnp.where(picked & (rank < room), rank, 2.0 * room).astype(BF16)
        fold_row = lax.broadcasted_iota(I32, (half, wide), 0)
        fold_col = lax.broadcasted_iota(I32, (half, wide), 1)
        fold = bits(fold_row // pad + ab * per == fold_col)
        ranks = jnp.where(slot_of, dot(from_src, rank), 0.0).astype(BF16)
        gates = jnp.where(slot_of, dot(from_src, marks.astype(BF16)), 0.0).astype(BF16)
        rank_cols = rank_cols + dot(ranks, fold)
        gate_cols = gate_cols + dot(gates, fold)
    rank_ref[...] = rank_cols.astype(BF16)
    gate_cols = gate_cols.astype(BF16)
    rank_rows = rank_cols.T[:8]
    slot_iota = lax.broadcasted_iota(I32, (room, lanes), 0).astype(F32)
    for m in range(n):
        pick_ref[m] = bits(rank_rows[m : m + 1, :] == slot_iota)
    gate_slots = dot(pick_ref[y], gate_cols)
    my_lane = lax.broadcasted_iota(I32, (room, wide), 1) == y
    gate_col = jnp.sum(jnp.where(my_lane, gate_slots, 0.0), axis=1, keepdims=True)

    def fan_copy(k, m, slot):
        src, dst = ((fan_dy, full_dy), (fan_x, full_x))[k]
        return rdma(
            src.at[m], dst.at[slot, :, my_cols], fan_ss.at[m, k], fan_rs.at[slot, k], peer(m)
        )

    def twin_copy(k, slot):
        buf = (full_dy, full_x)[k]
        return rdma(
            buf.at[slot, :, my_cols], buf.at[slot, :, my_cols],
            twin_ss.at[slot, k], twin_rs.at[slot, k], twin,
        )

    def twin_arrival(k, slot):
        buf = (full_dy, full_x)[k]
        return rdma(
            buf.at[slot, :, twin_cols], buf.at[slot, :, twin_cols],
            twin_ss.at[slot, k], twin_rs.at[slot, k], twin,
        )

    def landed(k):
        land = (l_dy, l_x)[k]

        def wait(i, _):
            for dx in range(1, NX):
                xx = (x + dx) % NX
                x_copy(k, xx, xx, i).wait_recv()
            return _

        lax.fori_loop(0, pairs, wait, 0)
        return land[...].reshape(lanes, wide)

    def spread(k):
        src, dst, rows = ((fan_dy, full_dy), (fan_x, full_x))[k] + (landed(k),)

        def one(i, _):
            m = (y + ring_offset(i, n)) % n
            out = dot(pick_ref[m], rows).astype(BF16)

            @pl.when(i < n - 1)
            def _far():
                src[m] = out
                fan_copy(k, m, y).start()

            @pl.when(i == n - 1)
            def _near():
                dst[y, :, my_cols] = out
                twin_copy(k, y).start()

            return _

        lax.fori_loop(0, n, one, 0)

    def source(i):
        return (y + n - ring_offset(i, n)) % n

    def hand_over(k, i):
        slot = source(i)
        fan_copy(k, slot, slot).wait_recv()
        twin_copy(k, slot).start()

    def columns(slot):
        return pl.ds(pl.multiple_of(slot * 2 * wide, 2 * wide), 2 * wide)

    spread(0)
    acc_g[...] = jnp.zeros_like(acc_g)
    acc_u[...] = jnp.zeros_like(acc_u)
    acc_b[...] = jnp.zeros_like(acc_b)

    def onward_x(i, _):
        onward(1, i)

        @pl.when(i < n - 1)
        def _dy():
            hand_over(0, jnp.minimum(i, n - 2))

        return _

    lax.fori_loop(0, pairs, onward_x, 0)
    for i in range(pairs, n - 1):
        hand_over(0, i)
    spread(1)
    loads[2].wait()

    def back_rows(slot, _):
        twin_arrival(0, slot).wait_recv()
        acc_b[...] += lax.dot_general(
            full_dy[slot], wd_ref[:, columns(slot)], NT, preferred_element_type=F32
        )
        return _

    lax.fori_loop(0, n, back_rows, 0)
    loads[0].wait()
    loads[1].wait()

    def multiply(slot):
        twin_arrival(1, slot).wait_recv()
        rows = columns(slot)
        xs = full_x[slot]
        acc_g[...] += dot(xs, wg_ref[rows, :])
        acc_u[...] += dot(xs, wu_ref[rows, :])

    def gather(i, _):
        hand_over(1, i)
        multiply(jnp.where(i == 0, y, source(jnp.maximum(i - 1, 0))))
        return _

    lax.fori_loop(0, n - 1, gather, 0)
    multiply(source(n - 2))

    g = acc_g[...]
    u = acc_u[...]
    b = acc_b[...]
    s = 1.0 / (1.0 + jnp.exp(-g))
    a = g * s
    q = gate_col * b
    dg_ref[...] = (q * u * (s * (1.0 + g * (1.0 - s)))).astype(BF16)
    du_ref[...] = (q * a).astype(BF16)
    gate_part = a * u * b
    high = gate_part.astype(BF16)
    low = (gate_part - high.astype(F32)).astype(BF16)
    ones = jnp.ones((8, gate_part.shape[1]), BF16)
    c_half = lax.dot_general(ones, high, NT, preferred_element_type=F32) + lax.dot_general(
        ones, low, NT, preferred_element_type=F32
    )
    c_own[...] = c_half.astype(BF16).astype(F32)
    rdma(c_own, c_got, cx_ss, cx_rs, twin).start()

    def give_copy(t):
        return rdma(give.at[t], got.at[t], give_ss.at[t], give_rs.at[t], twin)

    def ret_copy(t, slot):
        return rdma(pair.at[t], back.at[slot], ret_ss.at[t], ret_rs.at[slot], peer(t))

    def c_copy(t, slot):
        return rdma(c_all.at[y], c_all.at[slot], cr_ss.at[t], cr_rs.at[slot], peer(t))

    def target(i):
        return (y + ring_offset(i, n)) % n

    def add_pair(i):
        t = target(i)
        give_copy(t).wait_recv()
        total = (keep[t] + got[t].astype(F32)).astype(BF16)

        @pl.when(i < n - 1)
        def _far():
            pair[t] = total
            ret_copy(t, y).start()

        @pl.when(i == n - 1)
        def _near():
            back[y] = total

    def produce(i, _):
        t = target(i)
        rows = pl.ds(pl.multiple_of(t * 2 * wide, 2 * wide), 2 * wide)
        part = lax.dot_general(dg_ref[...], wg_ref[rows, :], NT, preferred_element_type=F32)
        part = part + lax.dot_general(du_ref[...], wu_ref[rows, :], NT, preferred_element_type=F32)
        left, right = part[:, :wide], part[:, wide:]
        keep[t] = jnp.where(core == 0, left, right)
        give[t] = jnp.where(core == 0, right, left).astype(BF16)
        give_copy(t).start()

        @pl.when(i > 0)
        def _before():
            add_pair(jnp.maximum(i - 1, 0))

        return _

    lax.fori_loop(0, n, produce, 0)
    rdma(c_own, c_got, cx_ss, cx_rs, twin).wait_recv()
    c_all[y] = (c_own[...] + c_got[...]).astype(BF16).astype(F32)

    def c_send(i, _):
        c_copy(target(i), y).start()
        return _

    lax.fori_loop(0, n - 1, c_send, 0)

    add_pair(n - 1)

    acc[...] = jnp.zeros_like(acc)
    lane_iota = lax.broadcasted_iota(I32, (lanes, room), 1).astype(F32)
    eye = lax.broadcasted_iota(I32, (room, room), 0) == lax.broadcasted_iota(I32, (room, room), 1)
    col_iota = lax.broadcasted_iota(I32, (room, wide), 1)
    pick_row = lax.broadcasted_iota(I32, (wide, room), 0)

    def combine(slot):
        rank = dot(rank_ref[...], bits(pick_row == slot))
        pick = bits(rank == lane_iota)
        c_col = jnp.sum(jnp.where(eye, c_all[slot][:1, :], 0.0), axis=1, keepdims=True)
        c_cols = jnp.where(col_iota == slot, c_col, 0.0).astype(BF16)
        acc[...] += dot(pick, jnp.concatenate([back[slot], c_cols], axis=1))

    combine(y)

    def collect(i, _):
        slot = source(i)
        ret_copy(slot, slot).wait_recv()
        c_copy(slot, slot).wait_recv()
        combine(slot)
        return _

    lax.fori_loop(0, n - 1, collect, 0)

    total = acc[:, :wide].astype(BF16).reshape(NX, nz * send, wide)
    lane_c = acc[:, wide:].astype(BF16)
    un_row = lax.broadcasted_iota(I32, (wide, half), 0)
    un_col = lax.broadcasted_iota(I32, (wide, half), 1)
    lane_to = lax.broadcasted_iota(I32, (n_grp, lanes), 1)
    src_to = lax.broadcasted_iota(I32, (n_grp, lanes), 0) * send
    to_src = bits((lane_to >= src_to) & (lane_to < src_to + send))

    def home_x(to, slot):
        return rdma(o_x.at[to], m_x.at[slot], hx_ss.at[to], hx_rs.at[slot], at_x(to))

    def both_z(slot):
        return pl.ds(pl.multiple_of(slot * 2 * nz, 8), 2 * nz)

    def home_c(to, slot):
        return rdma(o_c.at[to], m_c.at[both_z(slot)], hc_ss.at[to], hc_rs.at[slot], at_x(to))

    for xx in range(NX):

        @pl.when(xx != x)
        def _far():
            o_x[xx] = total[xx]
            home_x(xx, x).start()

        @pl.when(xx == x)
        def _near():
            m_x[xx] = total[xx]

    for ab in range(2):
        spread_c = dot(lane_c, bits(un_col // pad + ab * per == un_row))
        table = dot(to_src, jnp.where(slot_of, spread_c, 0.0).astype(BF16))
        for xx in range(NX):
            o_c[xx, ab * nz : (ab + 1) * nz, :] = table[xx * nz : (xx + 1) * nz]
    for dx in range(1, NX):
        home_c((x + dx) % NX, x).start()
    m_c[both_z(x)] = o_c[x]
    for dx in range(1, NX):
        xx = (x + dx) % NX
        home_x(xx, xx).wait_recv()
        home_c(xx, xx).wait_recv()

    def home_z(k, to, slot):
        src, dst = ((zo_x, h_x), (s_c, h_c))[k]
        return rdma(src.at[to], dst.at[slot], hz_ss.at[k, to], hz_rs.at[k, slot], at_z(to))

    def off(i, _):
        j = (z // 2 + ring_offset(i, pairs)) % pairs
        rows = pair_rows(j)
        parts = [m_x[xx, rows].astype(F32) for xx in range(NX)]
        for zz in range(2):
            to = 2 * j + zz
            zo_x[to] = jnp.concatenate(
                [part[zz * send : (zz + 1) * send] for part in parts], axis=0
            ).astype(BF16)
            for ab in range(2):
                s_c[to, ab * NX : (ab + 1) * NX, :] = m_c[
                    pl.ds(ab * nz + to, NX, 2 * nz), :
                ]

            @pl.when(to != z)
            def _far():
                home_z(0, to, z).start()
                home_z(1, to, z).start()

        return _

    lax.fori_loop(0, pairs, off, 0)
    h_x[z] = zo_x[z]
    h_c[z] = s_c[z]

    def home_in(i, _):
        slot = (z + i) % nz
        home_z(0, slot, slot).wait_recv()
        home_z(1, slot, slot).wait_recv()
        return _

    lax.fori_loop(1, nz, home_in, 0)
    out_x[...] = h_x[...]
    out_c[...] = h_c[...]

    def drain_z(i, _):
        to = (z + i) % nz
        for k in range(3):
            z_copy(k, to, z).wait_send()
        home_z(0, to, z).wait_send()
        home_z(1, to, z).wait_send()
        return _

    lax.fori_loop(1, nz, drain_z, 0)
    for dx in range(1, NX):
        to = (x + dx) % NX
        marks_copy(to, x).wait_send()
        home_x(to, x).wait_send()
        home_c(to, x).wait_send()

        def drain_x(j, _, to=to):
            x_copy(0, to, x, j).wait_send()
            x_copy(1, to, x, j).wait_send()
            return _

        lax.fori_loop(0, pairs, drain_x, 0)

    def drain_y(i, _):
        t = target(i)
        fan_copy(0, t, y).wait_send()
        fan_copy(1, t, y).wait_send()
        ret_copy(t, y).wait_send()
        c_copy(t, y).wait_send()
        return _

    lax.fori_loop(0, n - 1, drain_y, 0)

    def drain_twin(i, _):
        twin_copy(0, i).wait_send()
        twin_copy(1, i).wait_send()
        give_copy(i).wait_send()
        return _

    lax.fori_loop(0, n, drain_twin, 0)
    rdma(c_own, c_got, cx_ss, cx_rs, twin).wait_send()


def routed(sx, sdy, marks, wg, wu, wd, n, room):
    nz, chunk, wide = sx.shape
    lanes = nz * chunk
    hidden = wg.shape[1]
    pairs = nz // 2
    dma = pltpu.SemaphoreType.DMA
    block = (n, room, wide)
    by_x = (NX, lanes // NX, wide)
    vmem = pl.BlockSpec(memory_space=pltpu.VMEM)
    hbm = pl.BlockSpec(memory_space=pl.ANY)
    half = META // 2
    return pl.pallas_call(
        kernel,
        out_shape=(
            jax.ShapeDtypeStruct((nz, chunk, wide), BF16),
            jax.ShapeDtypeStruct((nz, 8, half), F32),
        ),
        in_specs=[vmem] * 3 + [hbm] * 3,
        out_specs=(vmem, vmem),
        scratch_shapes=[
            pltpu.VMEM(wg.shape, BF16),
            pltpu.VMEM(wu.shape, BF16),
            pltpu.VMEM(wd.shape, BF16),
            pltpu.VMEM(sx.shape, BF16),
            pltpu.VMEM(sx.shape, BF16),
            pltpu.VMEM((nz * 8, half), F32),
            pltpu.VMEM(by_x, BF16),
            pltpu.VMEM(by_x, BF16),
            pltpu.VMEM(by_x, BF16),
            pltpu.VMEM(by_x, BF16),
            pltpu.VMEM((NX * nz * 8, half), F32),
            pltpu.VMEM((n, room, lanes), BF16),
            pltpu.VMEM((lanes, wide), BF16),
            pltpu.VMEM(block, BF16),
            pltpu.VMEM(block, BF16),
            pltpu.VMEM((n, room, 2 * wide), BF16),
            pltpu.VMEM((n, room, 2 * wide), BF16),
            pltpu.VMEM((room, hidden), F32),
            pltpu.VMEM((room, hidden), F32),
            pltpu.VMEM((room, hidden), F32),
            pltpu.VMEM((room, hidden), BF16),
            pltpu.VMEM((room, hidden), BF16),
            pltpu.VMEM(block, F32),
            pltpu.VMEM(block, BF16),
            pltpu.VMEM(block, BF16),
            pltpu.VMEM(block, BF16),
            pltpu.VMEM(block, BF16),
            pltpu.VMEM((8, room), F32),
            pltpu.VMEM((8, room), F32),
            pltpu.VMEM((n, 8, room), F32),
            pltpu.VMEM((lanes, 2 * wide), F32),
            pltpu.VMEM(by_x, BF16),
            pltpu.VMEM(by_x, BF16),
            pltpu.VMEM(sx.shape, BF16),
            pltpu.VMEM((NX, 2 * nz, half), F32),
            pltpu.VMEM((NX * 2 * nz, half), F32),
            pltpu.VMEM((nz, 8, half), F32),
            pltpu.VMEM((nz, 8, half), F32),
            pltpu.VMEM(sx.shape, BF16),
            dma((3,)),
            dma((3, nz)),
            dma((3, nz)),
            dma((2, NX, pairs)),
            dma((2, NX, pairs)),
            dma((NX,)),
            dma((NX,)),
            dma((n, 2)),
            dma((n, 2)),
            dma((n, 2)),
            dma((n, 2)),
            dma((n,)),
            dma((n,)),
            dma((n,)),
            dma((n,)),
            dma,
            dma,
            dma((n,)),
            dma((n,)),
            dma((NX,)),
            dma((NX,)),
            dma((NX,)),
            dma((NX,)),
            dma((2, nz)),
            dma((2, nz)),
        ],
        compiler_params=pltpu.CompilerParams(
            collective_id=0, has_side_effects=True, vmem_limit_bytes=48 << 20
        ),
        cost_estimate=pl.CostEstimate(
            flops=10 * room * hidden * n * 2 * wide, bytes_accessed=8 << 20, transcendentals=0
        ),
    )(sx, sdy, marks, wg, wu, wd)


def shards(inputs, out_grad, expert_ids, gate_probs, group_slot, w_gate, w_up, w_down):
    n_grp = lax.axis_size("grp")
    n_loc = lax.axis_size("loc")
    exp_grp = n_loc // 2
    tok, wide = inputs.shape
    room = 2 * tok
    send = max(1, 3 * tok // 16)
    lanes = n_grp * send
    pad = META // exp_grp
    nz = n_grp // NX

    group = expert_ids // exp_grp
    member = expert_ids % exp_grp
    sent = group_slot < send
    order = group % nz * NX + group // nz
    lane = jnp.where(sent, order * send + group_slot, lanes)
    place = jnp.any(
        lane.T[None] == jnp.arange(lanes, dtype=I32)[:, None, None], axis=1
    ).astype(BF16)
    field = jnp.where(sent, member * pad + group_slot, META).reshape(-1)
    of_group = (order.reshape(-1)[None, :] == jnp.arange(n_grp, dtype=I32)[:, None]).astype(BF16)
    of_field = field[:, None] == jnp.arange(META, dtype=I32)[None, :]
    marks = dot(
        of_group, jnp.where(of_field, gate_probs.reshape(-1)[:, None], jnp.zeros((), BF16))
    )
    home_x, home_c = routed(
        dot(place, inputs).astype(BF16).reshape(nz, NX * send, wide),
        dot(place, out_grad).astype(BF16).reshape(nz, NX * send, wide),
        marks.reshape(nz, 2 * NX, META // 2),
        w_gate[0],
        w_up[0],
        w_down[0],
        exp_grp,
        room,
    )
    in_grad = lax.dot_general(
        place,
        home_x.reshape(lanes, wide),
        (((0,), (0,)), ((), ())),
        preferred_element_type=F32,
    ).astype(BF16)
    table = home_c.reshape(nz, 2, NX, META // 2).transpose(0, 2, 1, 3).reshape(n_grp, META)
    picks = lax.dot_general(
        of_group, table.astype(BF16), (((0,), (0,)), ((), ())), preferred_element_type=F32
    )
    gate_grad = jnp.sum(jnp.where(of_field, picks, 0.0), axis=1).astype(BF16)
    return in_grad, gate_grad.reshape(expert_ids.shape)


def solution(mesh):
    return jax.shard_map(
        shards,
        mesh=mesh,
        in_specs=(
            P("grp", "loc"),
            P("grp", "loc"),
            P("grp", None),
            P("grp", None),
            P("grp", None),
            P(("grp", "loc"), None, None),
            P(("grp", "loc"), None, None),
            P(("grp", "loc"), None, None),
        ),
        out_specs=(P("grp", "loc"), P("grp", None)),
        check_vma=False,
    )
```

```python
import jax
import jax.numpy as jnp
from jax import lax
from jax.experimental import pallas as pl
from jax.experimental.pallas import tpu as pltpu
from jax.sharding import PartitionSpec as P

MESH = pl.DeviceIdType.MESH
F32 = jnp.float32
BF16 = jnp.bfloat16
I32 = jnp.int32
NX = 4
META = 256
NT = (((1,), (1,)), ((), ()))


def dot(a, b):
    return jnp.dot(a, b, preferred_element_type=F32)


def bits(mask):
    return mask.astype(F32).astype(BF16)


def ring_offset(i, n):
    half = (i + 1) // 2
    return n // 2 + jnp.where(i % 2 == 0, half, -half)


def near_offset(i, n):
    half = (i + 1) // 2
    return jnp.where(i % 2 == 0, n - half, half) % n


def kernel(
    x_ref, dy_ref, marks_ref, wg_hbm, wu_hbm, wd_hbm,
    out_x, out_c,
    wg_ref, wu_ref, wd_ref,
    raw_dy, raw_x, z_marks, place_ref, x_dy, x_x, l_dy, l_x, x_marks, l_marks, y_marks,
    pick_ref, rank_ref, row_ref,
    fan_x, fan_dy, full_x, full_dy, acc_g, acc_u, acc_b, dg_ref, du_ref,
    keep, give, got, pair, back, gate_ref, c_own, c_got, c_all, acc,
    o_x, m_x, h_x, o_c, m_c, s_c, h_c, zo_x,
    w_sem, z_ss, z_rs, ag_ss, ag_rs, x_ss, x_rs, xm_ss, xm_rs, ym_ss, ym_rs,
    fan_ss, fan_rs, twin_ss, twin_rs, give_ss, give_rs, ret_ss, ret_rs,
    cx_ss, cx_rs, cr_ss, cr_rs, hx_ss, hx_rs, hc_ss, hc_rs, hz_ss, hz_rs,
):
    n = full_x.shape[0]
    room, wide = fan_x.shape[1:]
    nz, chunk = zo_x.shape[:2]
    tok = x_ref.shape[0]
    send = chunk // NX
    two = 2 * send
    pairs = nz // 2
    lanes = nz * chunk
    n_grp = NX * nz
    half = META // 2
    grp = lax.axis_index("grp")
    loc = lax.axis_index("loc")
    x, z = grp // nz, grp % nz
    y, core = loc // 2, loc % 2
    twin = (grp, 2 * y + 1 - core)
    my_cols = pl.ds(pl.multiple_of(core * wide, wide), wide)
    twin_cols = pl.ds(pl.multiple_of((1 - core) * wide, wide), wide)

    def rdma(src, dst, ss, rs, to):
        return pltpu.make_async_remote_copy(
            src_ref=src, dst_ref=dst, send_sem=ss, recv_sem=rs, device_id=to, device_id_type=MESH
        )

    def at_z(zz):
        return (x * nz + zz, loc)

    def at_x(xx):
        return (xx * nz + z, loc)

    def peer(yy):
        return (grp, 2 * yy + core)

    loads = [
        pltpu.make_async_copy(src, dst, w_sem.at[i])
        for i, (src, dst) in enumerate(((wg_hbm, wg_ref), (wu_hbm, wu_ref), (wd_hbm, wd_ref)))
    ]
    for load in loads:
        load.start()

    barrier = pltpu.get_barrier_semaphore()

    def greet(to):
        pl.semaphore_signal(barrier, inc=1, device_id=to, device_id_type=MESH)

    def greet_z(i, _):
        greet(at_z((z + i) % nz))
        return _

    def greet_y(i, _):
        greet(peer((y + i) % n))
        return _

    lax.fori_loop(1, nz, greet_z, 0)
    for dx in range(1, NX):
        greet(at_x((x + dx) % NX))
    lax.fori_loop(1, n, greet_y, 0)
    greet(twin)
    pl.semaphore_wait(barrier, nz - 1 + NX - 1 + n - 1 + 1)

    def eight(slot):
        return pl.ds(pl.multiple_of(slot * 8, 8), 8)

    def ag_copy(k, block, idx, hop):
        raw = (raw_dy, raw_x)[k]
        return rdma(
            raw.at[block], raw.at[block], ag_ss.at[k, idx], ag_rs.at[k, block],
            at_z((z + hop + nz) % nz),
        )

    def passes(k, away):
        if away == 0:
            return ((0, 3), (1, -3), (2, 1), (3, -1))
        sign = 1 if away > 0 else -1
        base = {3: 4, -3: 7, 6: 10, -6: 13}[away]
        hops = ((base, 3 * sign), (base + 1, sign), (base + 2, -sign))
        if abs(away) == 3:
            return hops
        last = ((base + 2, 2 * sign),) if k == (0 if sign > 0 else 1) else ()
        return ((base, sign), (base + 1, -sign)) + last

    def arrived(k, block):
        ag_copy(k, block, 0, 1).wait_recv()

    def pass_on(k, away):
        block = (z - away + nz) % nz
        if away != 0:
            arrived(k, block)
        for idx, hop in passes(k, away):
            ag_copy(k, block, idx, hop).start()

    def meta_copy(to, slot):
        return rdma(
            marks_ref.at[to], z_marks.at[eight(slot)], z_ss.at[to], z_rs.at[slot], at_z(to)
        )

    raw_dy[z] = dy_ref[...]
    pass_on(0, 0)

    def meta_send(i, _):
        meta_copy((z + ring_offset(i, nz)) % nz, z).start()
        return _

    lax.fori_loop(0, nz - 1, meta_send, 0)
    z_marks[eight(z)] = marks_ref[z]
    raw_x[z] = x_ref[...]
    for away in (3, -3):
        pass_on(0, away)
    pass_on(1, 0)

    def meta_in(i, _):
        meta_copy((z + i) % nz, (z + i) % nz).wait_recv()
        return _

    lax.fori_loop(1, nz, meta_in, 0)

    def all_z(slot):
        return pl.ds(pl.multiple_of(slot * nz, 8), nz)

    def marks_copy(to, slot):
        return rdma(x_marks, l_marks.at[all_z(slot)], xm_ss.at[to], xm_rs.at[slot], at_x(to))

    x_marks[...] = z_marks[pl.ds(NX, nz, 8), :]
    l_marks[all_z(x)] = x_marks[...]
    for dx in range(1, NX):
        marks_copy((x + dx) % NX, x).start()
    for k, away in ((0, 6), (0, -6), (1, 3), (1, -3)):
        pass_on(k, away)
    slot_rows = lax.broadcasted_iota(I32, (send, half), 0).astype(F32)

    def place(i, _):
        parts = [z_marks[pl.ds(i * 8 + xx, 1), :] == slot_rows for xx in range(NX)]
        place_ref[i] = bits(jnp.concatenate([part.astype(F32) for part in parts], axis=0) > 0.5)
        return _

    lax.fori_loop(0, nz, place, 0)
    for dx in range(1, NX):
        marks_copy((x + dx) % NX, (x + dx) % NX).wait_recv()
    pad = META // n
    per = half // pad
    part = half // NX
    take_row = lax.broadcasted_iota(I32, (half, half), 0)
    take_col = lax.broadcasted_iota(I32, (half, half), 1)
    inside = (take_row >= x * part) & (take_row < x * part + part)
    take = bits(inside & (take_row - x * part == take_col - (y % per) * pad))
    y_marks[y] = dot(l_marks[...].astype(BF16), take).astype(BF16)

    def gates_copy(to, slot):
        return rdma(y_marks.at[y], y_marks.at[slot], ym_ss.at[to], ym_rs.at[slot], peer(to))

    def gates_send(i, _):
        gates_copy((y + ring_offset(i, n)) % n, y).start()
        return _

    lax.fori_loop(0, n - 1, gates_send, 0)

    def pair_rows(j):
        return pl.ds(pl.multiple_of(j * two, 16 if two % 16 == 0 else 1), two)

    def x_copy(k, to, slot, j):
        src, dst = ((x_dy, l_dy), (x_x, l_x))[k]
        rows = pair_rows(j)
        return rdma(
            src.at[to, rows], dst.at[slot, rows], x_ss.at[k, to, j], x_rs.at[k, slot, j], at_x(to)
        )

    def onward(k, i):
        raw, out, land = ((raw_dy, x_dy, l_dy), (raw_x, x_x, l_x))[k]
        j = (z // 2 + near_offset(i, pairs)) % pairs
        chosen = []
        for zz in range(2):
            slot = 2 * j + zz
            away = (z - slot + nz) % nz
            passed = (away == 0) | (away == 3) | (away == 6) | (away == nz - 3) | (away == nz - 6)

            @pl.when(jnp.logical_not(passed))
            def _arrival():
                arrived(k, slot)

            chosen.append(dot(place_ref[slot][:, :tok], raw[slot]))
        even, odd = chosen
        rows = pair_rows(j)
        for xx in range(NX):
            mine = slice(xx * send, (xx + 1) * send)
            both = jnp.concatenate([even[mine], odd[mine]], axis=0).astype(BF16)

            @pl.when(xx != x)
            def _far():
                out[xx, rows] = both
                x_copy(k, xx, x, j).start()

            @pl.when(xx == x)
            def _near():
                land[xx, rows] = both

    def gates_in(i, _):
        slot = (y + i) % n
        gates_copy(slot, slot).wait_recv()
        return _

    lax.fori_loop(1, n, gates_in, 0)
    f_row = lax.broadcasted_iota(I32, (half, half), 0)
    f_col = lax.broadcasted_iota(I32, (half, half), 1)
    same = f_row // pad == f_col // pad
    upto = bits(same & (f_row <= f_col))
    block = bits(same)
    earlier = bits(
        lax.broadcasted_iota(I32, (n_grp, n_grp), 1) < lax.broadcasted_iota(I32, (n_grp, n_grp), 0)
    )
    lane_of = lax.broadcasted_iota(I32, (lanes, n_grp), 0)
    src_of = lax.broadcasted_iota(I32, (lanes, n_grp), 1) * send
    from_src = bits((lane_of >= src_of) & (lane_of < src_of + send))
    lane_f = lax.broadcasted_iota(I32, (lanes, half), 0)
    col_f = lax.broadcasted_iota(I32, (lanes, half), 1)
    slot_of = (col_f % pad) == (lane_f % send)
    rank_cols = jnp.zeros((lanes, wide), F32)
    gate_cols = jnp.zeros((lanes, wide), F32)
    for ab in range(2):
        marks = y_marks[ab * per].astype(F32)
        for m in range(1, per):
            marks = marks + y_marks[ab * per + m].astype(F32)
        picked = marks != 0.0
        count = bits(picked)
        within = dot(count, upto)
        before = dot(earlier, dot(count, block).astype(BF16))
        rank = within + before - 1.0
        rank = jnp.where(picked & (rank < room), rank, 2.0 * room).astype(BF16)
        fold_row = lax.broadcasted_iota(I32, (half, wide), 0)
        fold_col = lax.broadcasted_iota(I32, (half, wide), 1)
        fold = bits(fold_row // pad + ab * per == fold_col)
        ranks = jnp.where(slot_of, dot(from_src, rank), 0.0).astype(BF16)
        gates = jnp.where(slot_of, dot(from_src, marks.astype(BF16)), 0.0).astype(BF16)
        rank_cols = rank_cols + dot(ranks, fold)
        gate_cols = gate_cols + dot(gates, fold)
    for away in (6, -6):
        pass_on(1, away)
    def onward_dy(i, _):
        onward(0, i)
        return _

    lax.fori_loop(0, pairs, onward_dy, 0)
    rank_ref[...] = rank_cols.astype(BF16)
    gate_cols = gate_cols.astype(BF16)
    row_ref[...] = rank_cols.T[:8]
    slot_iota = lax.broadcasted_iota(I32, (room, lanes), 0).astype(F32)
    def fan_copy(k, m, slot):
        src, dst = ((fan_dy, full_dy), (fan_x, full_x))[k]
        return rdma(
            src.at[m], dst.at[slot, :, my_cols], fan_ss.at[m, k], fan_rs.at[slot, k], peer(m)
        )

    def twin_copy(k, slot):
        buf = (full_dy, full_x)[k]
        return rdma(
            buf.at[slot, :, my_cols], buf.at[slot, :, my_cols],
            twin_ss.at[slot, k], twin_rs.at[slot, k], twin,
        )

    def twin_arrival(k, slot):
        buf = (full_dy, full_x)[k]
        return rdma(
            buf.at[slot, :, twin_cols], buf.at[slot, :, twin_cols],
            twin_ss.at[slot, k], twin_rs.at[slot, k], twin,
        )

    def landed(k):
        land = (l_dy, l_x)[k]

        def wait(i, _):
            for dx in range(1, NX):
                xx = (x + dx) % NX
                x_copy(k, xx, xx, i).wait_recv()
            return _

        lax.fori_loop(0, pairs, wait, 0)
        return land[...].reshape(lanes, wide)

    def spread(k):
        src, dst, rows = ((fan_dy, full_dy), (fan_x, full_x))[k] + (landed(k),)

        def one(i, _):
            m = (y + ring_offset(i, n)) % n
            if k == 0:
                pick_ref[m] = bits(row_ref[pl.ds(m, 1), :] == slot_iota)
            out = dot(pick_ref[m], rows).astype(BF16)

            @pl.when(i < n - 1)
            def _far():
                src[m] = out
                fan_copy(k, m, y).start()

            @pl.when(i == n - 1)
            def _near():
                dst[y, :, my_cols] = out
                twin_copy(k, y).start()

            return _

        lax.fori_loop(0, n, one, 0)

    def source(i):
        return (y + n - ring_offset(i, n)) % n

    def hand_over(k, i):
        slot = source(i)
        fan_copy(k, slot, slot).wait_recv()
        twin_copy(k, slot).start()

    def columns(slot):
        return pl.ds(pl.multiple_of(slot * 2 * wide, 2 * wide), 2 * wide)

    spread(0)
    gate_slots = dot(pick_ref[y], gate_cols)
    my_lane = lax.broadcasted_iota(I32, (room, wide), 1) == y
    gate_col = jnp.sum(jnp.where(my_lane, gate_slots, 0.0), axis=1, keepdims=True)
    acc_g[...] = jnp.zeros_like(acc_g)
    acc_u[...] = jnp.zeros_like(acc_u)
    acc_b[...] = jnp.zeros_like(acc_b)

    def onward_x(i, _):
        onward(1, i)

        @pl.when(i < n - 1)
        def _dy():
            hand_over(0, jnp.minimum(i, n - 2))

        return _

    lax.fori_loop(0, pairs, onward_x, 0)
    for i in range(pairs, n - 1):
        hand_over(0, i)
    spread(1)
    loads[2].wait()

    def back_rows(slot, _):
        twin_arrival(0, slot).wait_recv()
        acc_b[...] += lax.dot_general(
            full_dy[slot], wd_ref[:, columns(slot)], NT, preferred_element_type=F32
        )
        return _

    lax.fori_loop(0, n, back_rows, 0)
    loads[0].wait()
    loads[1].wait()

    def multiply(slot):
        twin_arrival(1, slot).wait_recv()
        rows = columns(slot)
        xs = full_x[slot]
        acc_g[...] += dot(xs, wg_ref[rows, :])
        acc_u[...] += dot(xs, wu_ref[rows, :])

    def gather(i, _):
        hand_over(1, i)
        multiply(jnp.where(i == 0, y, source(jnp.maximum(i - 1, 0))))
        return _

    lax.fori_loop(0, n - 1, gather, 0)
    multiply(source(n - 2))

    g = acc_g[...]
    u = acc_u[...]
    b = acc_b[...]
    s = 1.0 / (1.0 + jnp.exp(-g))
    a = g * s
    q = gate_col * b
    dg_ref[...] = (q * u * (s * (1.0 + g * (1.0 - s)))).astype(BF16)
    du_ref[...] = (q * a).astype(BF16)
    gate_ref[...] = a * u * b

    def give_copy(t):
        return rdma(give.at[t], got.at[t], give_ss.at[t], give_rs.at[t], twin)

    def ret_copy(t, slot):
        return rdma(pair.at[t], back.at[slot], ret_ss.at[t], ret_rs.at[slot], peer(t))

    def target(i):
        return (y + ring_offset(i, n)) % n

    def add_pair(i):
        t = target(i)
        give_copy(t).wait_recv()
        total = (keep[t] + got[t].astype(F32)).astype(BF16)

        @pl.when(i < n - 1)
        def _far():
            pair[t] = total
            ret_copy(t, y).start()

        @pl.when(i == n - 1)
        def _near():
            back[y] = total

    def produce(i, _):
        t = target(i)
        rows = pl.ds(pl.multiple_of(t * 2 * wide, 2 * wide), 2 * wide)
        part = lax.dot_general(dg_ref[...], wg_ref[rows, :], NT, preferred_element_type=F32)
        part = part + lax.dot_general(du_ref[...], wu_ref[rows, :], NT, preferred_element_type=F32)
        left, right = part[:, :wide], part[:, wide:]
        keep[t] = jnp.where(core == 0, left, right)
        give[t] = jnp.where(core == 0, right, left).astype(BF16)
        give_copy(t).start()

        @pl.when(i > 0)
        def _before():
            add_pair(jnp.maximum(i - 1, 0))

        return _

    lax.fori_loop(0, n, produce, 0)
    add_pair(n - 1)
    gate_part = gate_ref[...]
    high = gate_part.astype(BF16)
    low = (gate_part - high.astype(F32)).astype(BF16)
    ones = jnp.ones((8, gate_part.shape[1]), BF16)
    c_half = lax.dot_general(ones, high, NT, preferred_element_type=F32) + lax.dot_general(
        ones, low, NT, preferred_element_type=F32
    )
    c_own[...] = c_half.astype(BF16).astype(F32)
    rdma(c_own, c_got, cx_ss, cx_rs, twin).start()

    acc[...] = jnp.zeros_like(acc)
    lane_iota = lax.broadcasted_iota(I32, (lanes, room), 1).astype(F32)
    pick_row = lax.broadcasted_iota(I32, (wide, room), 0)

    def combine(slot):
        rank = dot(rank_ref[...], bits(pick_row == slot))
        pick = bits(rank == lane_iota)
        acc[...] += dot(pick, back[slot])

    combine(y)

    rdma(c_own, c_got, cx_ss, cx_rs, twin).wait_recv()
    c_lane = dot((c_own[...] + c_got[...]).astype(BF16), pick_ref[y])[:1, :]
    lane_to = lax.broadcasted_iota(I32, (n_grp, lanes), 1)
    src_to = lax.broadcasted_iota(I32, (n_grp, lanes), 0) * send
    c_rows = jnp.where((lane_to >= src_to) & (lane_to < src_to + send), c_lane, 0.0)
    c_spot = bits(col_f - x * part == lane_f % send)
    table = dot(c_rows.astype(BF16), c_spot)
    for xx in range(NX):
        o_c[xx] = table[xx * nz : (xx + 1) * nz]

    def home_c(to, slot):
        return rdma(o_c.at[to], m_c.at[slot], hc_ss.at[to], hc_rs.at[slot], at_x(to))

    for dx in range(1, NX):
        home_c((x + dx) % NX, x).start()

    def collect(i, _):
        slot = source(i)
        ret_copy(slot, slot).wait_recv()
        combine(slot)
        return _

    lax.fori_loop(0, n - 1, collect, 0)

    total = acc[...].astype(BF16).reshape(NX, nz * send, wide)
    def home_x(to, slot, j):
        rows = pair_rows(j)
        return rdma(
            o_x.at[to, rows], m_x.at[slot, rows], hx_ss.at[to, j], hx_rs.at[slot, j], at_x(to)
        )

    for xx in range(NX):

        @pl.when(xx != x)
        def _far():
            o_x[xx] = total[xx]

        @pl.when(xx == x)
        def _near():
            m_x[xx] = total[xx]

    def home_order(i):
        return (z // 2 + ring_offset(i, pairs)) % pairs

    def home_send(i, _):
        for dx in range(1, NX):
            home_x((x + dx) % NX, x, home_order(i)).start()
        return _

    lax.fori_loop(0, pairs, home_send, 0)

    def home_z(k, to, slot):
        src, dst = ((zo_x, h_x), (s_c, h_c))[k]
        return rdma(src.at[to], dst.at[slot], hz_ss.at[k, to], hz_rs.at[k, slot], at_z(to))

    for dx in range(1, NX):
        xx = (x + dx) % NX
        home_c(xx, xx).wait_recv()
    merged = o_c[x]
    for dx in range(1, NX):
        merged = merged + m_c[(x + dx) % NX]
    for zz in range(nz):
        s_c[zz] = merged[zz : zz + 1]

    def off_c(i, _):
        home_z(1, (z + ring_offset(i, nz)) % nz, z).start()
        return _

    lax.fori_loop(0, nz - 1, off_c, 0)

    def off(i, _):
        j = home_order(i)
        rows = pair_rows(j)
        for dx in range(1, NX):
            xx = (x + dx) % NX
            home_x(xx, xx, j).wait_recv()
        parts = [m_x[xx, rows].astype(F32) for xx in range(NX)]
        for zz in range(2):
            to = 2 * j + zz
            zo_x[to] = jnp.concatenate(
                [part[zz * send : (zz + 1) * send] for part in parts], axis=0
            ).astype(BF16)

            @pl.when(to != z)
            def _far():
                home_z(0, to, z).start()

        return _

    lax.fori_loop(0, pairs, off, 0)
    h_x[z] = zo_x[z]
    h_c[z] = s_c[z]

    def home_in(k):
        def one(i, _):
            slot = (z + i) % nz
            home_z(k, slot, slot).wait_recv()
            return _

        lax.fori_loop(1, nz, one, 0)

    home_in(1)
    for zz in range(nz):
        c_all[y, zz : zz + 1, :] = h_c[zz]

    def c_copy(t, slot):
        return rdma(c_all.at[y], c_all.at[slot], cr_ss.at[t], cr_rs.at[slot], peer(t))

    def c_send(i, _):
        c_copy(target(i), y).start()
        return _

    lax.fori_loop(0, n - 1, c_send, 0)
    home_in(0)

    def c_in(i, _):
        c_copy(source(i), source(i)).wait_recv()
        return _

    lax.fori_loop(0, n - 1, c_in, 0)
    out_x[...] = h_x[...]
    out_c[...] = c_all[...]

    def drain_z(i, _):
        to = (z + i) % nz
        meta_copy(to, z).wait_send()
        home_z(0, to, z).wait_send()
        home_z(1, to, z).wait_send()
        return _

    lax.fori_loop(1, nz, drain_z, 0)
    for dx in range(1, NX):
        to = (x + dx) % NX
        marks_copy(to, x).wait_send()
        home_c(to, x).wait_send()

        def drain_x(j, _, to=to):
            x_copy(0, to, x, j).wait_send()
            x_copy(1, to, x, j).wait_send()
            home_x(to, x, j).wait_send()
            return _

        lax.fori_loop(0, pairs, drain_x, 0)

    for k in range(2):
        for away in (0, 3, -3, 6, -6):
            for idx, hop in passes(k, away):
                ag_copy(k, z, idx, hop).wait_send()

    def drain_y(i, _):
        t = target(i)
        gates_copy(t, y).wait_send()
        fan_copy(0, t, y).wait_send()
        fan_copy(1, t, y).wait_send()
        ret_copy(t, y).wait_send()
        c_copy(t, y).wait_send()
        return _

    lax.fori_loop(0, n - 1, drain_y, 0)

    def drain_twin(i, _):
        twin_copy(0, i).wait_send()
        twin_copy(1, i).wait_send()
        give_copy(i).wait_send()
        return _

    lax.fori_loop(0, n, drain_twin, 0)
    rdma(c_own, c_got, cx_ss, cx_rs, twin).wait_send()


def routed(x, dy, marks, wg, wu, wd, n, room, send):
    nz = marks.shape[0]
    tok, wide = x.shape
    chunk = NX * send
    lanes = nz * chunk
    tokens = (nz, tok, wide)
    packed = (nz, chunk, wide)
    hidden = wg.shape[1]
    pairs = nz // 2
    dma = pltpu.SemaphoreType.DMA
    block = (n, room, wide)
    by_x = (NX, lanes // NX, wide)
    vmem = pl.BlockSpec(memory_space=pltpu.VMEM)
    hbm = pl.BlockSpec(memory_space=pl.ANY)
    half = META // 2
    return pl.pallas_call(
        kernel,
        out_shape=(
            jax.ShapeDtypeStruct(packed, BF16),
            jax.ShapeDtypeStruct((n, nz, half), F32),
        ),
        in_specs=[vmem] * 3 + [hbm] * 3,
        out_specs=(vmem, vmem),
        scratch_shapes=[
            pltpu.VMEM(wg.shape, BF16),
            pltpu.VMEM(wu.shape, BF16),
            pltpu.VMEM(wd.shape, BF16),
            pltpu.VMEM(tokens, BF16),
            pltpu.VMEM(tokens, BF16),
            pltpu.VMEM((nz * 8, half), F32),
            pltpu.VMEM((nz, chunk, half), BF16),
            pltpu.VMEM(by_x, BF16),
            pltpu.VMEM(by_x, BF16),
            pltpu.VMEM(by_x, BF16),
            pltpu.VMEM(by_x, BF16),
            pltpu.VMEM((nz, half), F32),
            pltpu.VMEM((NX * nz, half), F32),
            pltpu.VMEM((n, NX * nz, half), BF16),
            pltpu.VMEM((n, room, lanes), BF16),
            pltpu.VMEM((lanes, wide), BF16),
            pltpu.VMEM((8, lanes), F32),
            pltpu.VMEM(block, BF16),
            pltpu.VMEM(block, BF16),
            pltpu.VMEM((n, room, 2 * wide), BF16),
            pltpu.VMEM((n, room, 2 * wide), BF16),
            pltpu.VMEM((room, hidden), F32),
            pltpu.VMEM((room, hidden), F32),
            pltpu.VMEM((room, hidden), F32),
            pltpu.VMEM((room, hidden), BF16),
            pltpu.VMEM((room, hidden), BF16),
            pltpu.VMEM(block, F32),
            pltpu.VMEM(block, BF16),
            pltpu.VMEM(block, BF16),
            pltpu.VMEM(block, BF16),
            pltpu.VMEM(block, BF16),
            pltpu.VMEM((room, hidden), F32),
            pltpu.VMEM((8, room), F32),
            pltpu.VMEM((8, room), F32),
            pltpu.VMEM((n, nz, half), F32),
            pltpu.VMEM((lanes, wide), F32),
            pltpu.VMEM(by_x, BF16),
            pltpu.VMEM(by_x, BF16),
            pltpu.VMEM(packed, BF16),
            pltpu.VMEM((NX, nz, half), F32),
            pltpu.VMEM((NX, nz, half), F32),
            pltpu.VMEM((nz, 1, half), F32),
            pltpu.VMEM((nz, 1, half), F32),
            pltpu.VMEM(packed, BF16),
            dma((3,)),
            dma((nz,)),
            dma((nz,)),
            dma((2, 16)),
            dma((2, nz)),
            dma((2, NX, pairs)),
            dma((2, NX, pairs)),
            dma((NX,)),
            dma((NX,)),
            dma((n,)),
            dma((n,)),
            dma((n, 2)),
            dma((n, 2)),
            dma((n, 2)),
            dma((n, 2)),
            dma((n,)),
            dma((n,)),
            dma((n,)),
            dma((n,)),
            dma,
            dma,
            dma((n,)),
            dma((n,)),
            dma((NX, pairs)),
            dma((NX, pairs)),
            dma((NX,)),
            dma((NX,)),
            dma((2, nz)),
            dma((2, nz)),
        ],
        compiler_params=pltpu.CompilerParams(
            collective_id=0, has_side_effects=True, vmem_limit_bytes=48 << 20
        ),
        cost_estimate=pl.CostEstimate(
            flops=10 * room * hidden * n * 2 * wide, bytes_accessed=8 << 20, transcendentals=0
        ),
    )(x, dy, marks, wg, wu, wd)


def shards(inputs, out_grad, expert_ids, gate_probs, group_slot, w_gate, w_up, w_down):
    n_grp = lax.axis_size("grp")
    n_loc = lax.axis_size("loc")
    exp_grp = n_loc // 2
    tok, wide = inputs.shape
    room = 2 * tok
    send = max(1, 3 * tok // 16)
    lanes = n_grp * send
    nz = n_grp // NX
    part = META // 2 // NX

    group = expert_ids // exp_grp
    member = expert_ids % exp_grp
    sent = group_slot < send
    order = group % nz * NX + group // nz
    lane = jnp.where(sent, order * send + group_slot, lanes)
    place = jnp.any(
        lane.T[None] == jnp.arange(lanes, dtype=I32)[:, None, None], axis=1
    ).astype(BF16)
    field = jnp.where(sent, member * part + group_slot, exp_grp * part).reshape(-1)
    of_group = (order.reshape(-1)[None, :] == jnp.arange(n_grp, dtype=I32)[:, None]).astype(BF16)
    of_field = field[:, None] == jnp.arange(exp_grp * part, dtype=I32)[None, :]
    here = sent & (member == lax.axis_index("loc") // 2)
    own = jnp.where(here, group_slot, META).reshape(-1)[:, None]
    own = own == jnp.arange(part, dtype=I32)[None, :]
    marks = dot(
        of_group, jnp.where(own, gate_probs.reshape(-1)[:, None], jnp.zeros((), BF16))
    ).reshape(nz, 1, META // 2)
    spots = jnp.where(
        (order.T[None] == jnp.arange(n_grp, dtype=I32)[:, None, None]) & sent.T[None],
        group_slot.T[None],
        META,
    )
    spots = jnp.min(spots, axis=1).astype(F32).reshape(nz, NX, tok)
    spots = jnp.pad(spots, ((0, 0), (0, 0), (0, META // 2 - tok)), constant_values=META)
    meta = jnp.concatenate([spots, marks, jnp.zeros((nz, 7 - NX, META // 2), F32)], axis=1)
    home_x, home_c = routed(
        inputs,
        out_grad,
        meta,
        w_gate[0],
        w_up[0],
        w_down[0],
        exp_grp,
        room,
        send,
    )
    in_grad = lax.dot_general(
        place,
        home_x.reshape(lanes, wide),
        (((0,), (0,)), ((), ())),
        preferred_element_type=F32,
    ).astype(BF16)
    table = home_c.reshape(exp_grp, nz, NX, part).transpose(1, 2, 0, 3).reshape(n_grp, -1)
    picks = lax.dot_general(
        of_group, table.astype(BF16), (((0,), (0,)), ((), ())), preferred_element_type=F32
    )
    gate_grad = jnp.sum(jnp.where(of_field, picks, 0.0), axis=1).astype(BF16)
    return in_grad, gate_grad.reshape(expert_ids.shape)


def solution(mesh):
    return jax.shard_map(
        shards,
        mesh=mesh,
        in_specs=(
            P("grp", "loc"),
            P("grp", "loc"),
            P("grp", None),
            P("grp", None),
            P("grp", None),
            P(("grp", "loc"), None, None),
            P(("grp", "loc"), None, None),
            P(("grp", "loc"), None, None),
        ),
        out_specs=(P("grp", "loc"), P("grp", None)),
        check_vma=False,
    )
```

```python
import jax
import jax.numpy as jnp
from jax import lax
from jax.experimental import pallas as pl
from jax.experimental.pallas import tpu as pltpu
from jax.sharding import PartitionSpec as P

MESH = pl.DeviceIdType.MESH
F32 = jnp.float32
BF16 = jnp.bfloat16
I32 = jnp.int32
NX = 4
META = 256
NT = (((1,), (1,)), ((), ()))


def dot(a, b):
    return jnp.dot(a, b, preferred_element_type=F32)


def bits(mask):
    return mask.astype(F32).astype(BF16)


def ring_offset(i, n):
    half = (i + 1) // 2
    return n // 2 + jnp.where(i % 2 == 0, half, -half)


def near_offset(i, n):
    half = (i + 1) // 2
    return jnp.where(i % 2 == 0, n - half, half) % n


def kernel(
    x_ref, dy_ref, marks_ref, wg_hbm, wu_hbm, wd_hbm,
    out_x, out_c,
    wg_ref, wu_ref, wd_ref,
    raw_dy, raw_x, z_marks, place_ref, x_dy, x_x, l_dy, l_x, x_marks, l_marks, y_marks,
    pick_ref, rank_ref, row_ref,
    fan_x, fan_dy, full_x, full_dy, acc_g, acc_u, acc_b, dg_ref, du_ref,
    keep, give, got, pair, back, gate_ref, c_own, c_got, c_all, acc,
    o_x, m_x, h_x, o_c, m_c, s_c, h_c, zo_x,
    w_sem, z_ss, z_rs, ag_ss, ag_rs, x_ss, x_rs, xm_ss, xm_rs, ym_ss, ym_rs,
    fan_ss, fan_rs, twin_ss, twin_rs, give_ss, give_rs, ret_ss, ret_rs,
    cx_ss, cx_rs, cr_ss, cr_rs, hx_ss, hx_rs, hc_ss, hc_rs, hz_ss, hz_rs,
):
    n = full_x.shape[0]
    room, wide = fan_x.shape[1:]
    nz, chunk = zo_x.shape[:2]
    tok = x_ref.shape[0]
    send = chunk // NX
    two = 2 * send
    pairs = nz // 2
    lanes = nz * chunk
    n_grp = NX * nz
    half = META // 2
    grp = lax.axis_index("grp")
    loc = lax.axis_index("loc")
    x, z = grp // nz, grp % nz
    y, core = loc // 2, loc % 2
    twin = (grp, 2 * y + 1 - core)
    my_cols = pl.ds(pl.multiple_of(core * wide, wide), wide)
    twin_cols = pl.ds(pl.multiple_of((1 - core) * wide, wide), wide)

    def rdma(src, dst, ss, rs, to):
        return pltpu.make_async_remote_copy(
            src_ref=src, dst_ref=dst, send_sem=ss, recv_sem=rs, device_id=to, device_id_type=MESH
        )

    def at_z(zz):
        return (x * nz + zz, loc)

    def at_x(xx):
        return (xx * nz + z, loc)

    def peer(yy):
        return (grp, 2 * yy + core)

    loads = [
        pltpu.make_async_copy(src, dst, w_sem.at[i])
        for i, (src, dst) in enumerate(((wg_hbm, wg_ref), (wu_hbm, wu_ref), (wd_hbm, wd_ref)))
    ]
    for load in loads:
        load.start()

    barrier = pltpu.get_barrier_semaphore()

    def greet(to):
        pl.semaphore_signal(barrier, inc=1, device_id=to, device_id_type=MESH)

    def greet_z(i, _):
        greet(at_z((z + i) % nz))
        return _

    def greet_y(i, _):
        greet(peer((y + i) % n))
        return _

    lax.fori_loop(1, nz, greet_z, 0)
    for dx in range(1, NX):
        greet(at_x((x + dx) % NX))
    lax.fori_loop(1, n, greet_y, 0)
    greet(twin)
    pl.semaphore_wait(barrier, nz - 1 + NX - 1 + n - 1 + 1)

    def eight(slot):
        return pl.ds(pl.multiple_of(slot * 8, 8), 8)

    def ag_copy(k, block, idx, hop):
        raw = (raw_dy, raw_x)[k]
        return rdma(
            raw.at[block], raw.at[block], ag_ss.at[k, idx], ag_rs.at[k, block],
            at_z((z + hop + nz) % nz),
        )

    def passes(k, away):
        if away == 0:
            return ((0, 3), (1, -3), (2, 1), (3, -1))
        sign = 1 if away > 0 else -1
        base = {3: 4, -3: 7, 6: 10, -6: 13}[away]
        hops = ((base, 3 * sign), (base + 1, sign), (base + 2, -sign))
        if abs(away) == 3:
            return hops
        last = ((base + 2, 2 * sign),) if k == (0 if sign > 0 else 1) else ()
        return ((base, sign), (base + 1, -sign)) + last

    def arrived(k, block):
        ag_copy(k, block, 0, 1).wait_recv()

    def pass_on(k, away):
        block = (z - away + nz) % nz
        if away != 0:
            arrived(k, block)
        for idx, hop in passes(k, away):
            ag_copy(k, block, idx, hop).start()

    def meta_copy(to, slot):
        return rdma(
            marks_ref.at[to], z_marks.at[eight(slot)], z_ss.at[to], z_rs.at[slot], at_z(to)
        )

    raw_dy[z] = dy_ref[...]
    pass_on(0, 0)

    def meta_send(i, _):
        meta_copy((z + ring_offset(i, nz)) % nz, z).start()
        return _

    lax.fori_loop(0, nz - 1, meta_send, 0)
    z_marks[eight(z)] = marks_ref[z]
    raw_x[z] = x_ref[...]
    for away in (3, -3):
        pass_on(0, away)
    pass_on(1, 0)

    def meta_in(i, _):
        meta_copy((z + i) % nz, (z + i) % nz).wait_recv()
        return _

    lax.fori_loop(1, nz, meta_in, 0)

    def all_z(slot):
        return pl.ds(pl.multiple_of(slot * nz, 8), nz)

    def marks_copy(to, slot):
        return rdma(x_marks, l_marks.at[all_z(slot)], xm_ss.at[to], xm_rs.at[slot], at_x(to))

    x_marks[...] = z_marks[pl.ds(NX, nz, 8), :]
    l_marks[all_z(x)] = x_marks[...]
    for dx in range(1, NX):
        marks_copy((x + dx) % NX, x).start()
    for k, away in ((0, 6), (0, -6), (1, 3), (1, -3)):
        pass_on(k, away)
    slot_rows = lax.broadcasted_iota(I32, (send, half), 0).astype(F32)

    def place(i, _):
        parts = [z_marks[pl.ds(i * 8 + xx, 1), :] == slot_rows for xx in range(NX)]
        place_ref[i] = bits(jnp.concatenate([part.astype(F32) for part in parts], axis=0) > 0.5)
        return _

    lax.fori_loop(0, nz, place, 0)
    for dx in range(1, NX):
        marks_copy((x + dx) % NX, (x + dx) % NX).wait_recv()
    pad = META // n
    per = half // pad
    part = half // NX
    take_row = lax.broadcasted_iota(I32, (half, half), 0)
    take_col = lax.broadcasted_iota(I32, (half, half), 1)
    inside = (take_row >= x * part) & (take_row < x * part + part)
    take = bits(inside & (take_row - x * part == take_col - (y % per) * pad))
    y_marks[y] = dot(l_marks[...].astype(BF16), take).astype(BF16)

    def gates_copy(to, slot):
        return rdma(y_marks.at[y], y_marks.at[slot], ym_ss.at[to], ym_rs.at[slot], peer(to))

    def gates_send(i, _):
        gates_copy((y + ring_offset(i, n)) % n, y).start()
        return _

    lax.fori_loop(0, n - 1, gates_send, 0)

    def pair_rows(j):
        return pl.ds(pl.multiple_of(j * two, 16 if two % 16 == 0 else 1), two)

    def x_copy(k, to, slot, j):
        src, dst = ((x_dy, l_dy), (x_x, l_x))[k]
        rows = pair_rows(j)
        return rdma(
            src.at[to, rows], dst.at[slot, rows], x_ss.at[k, to, j], x_rs.at[k, slot, j], at_x(to)
        )

    def onward(k, i):
        raw, out, land = ((raw_dy, x_dy, l_dy), (raw_x, x_x, l_x))[k]
        j = (z // 2 + near_offset(i, pairs)) % pairs
        chosen = []
        for zz in range(2):
            slot = 2 * j + zz
            away = (z - slot + nz) % nz
            passed = (away == 0) | (away == 3) | (away == 6) | (away == nz - 3) | (away == nz - 6)

            @pl.when(jnp.logical_not(passed))
            def _arrival():
                arrived(k, slot)

            chosen.append(dot(place_ref[slot][:, :tok], raw[slot]))
        even, odd = chosen
        rows = pair_rows(j)
        for xx in range(NX):
            mine = slice(xx * send, (xx + 1) * send)
            both = jnp.concatenate([even[mine], odd[mine]], axis=0).astype(BF16)

            @pl.when(xx != x)
            def _far():
                out[xx, rows] = both
                x_copy(k, xx, x, j).start()

            @pl.when(xx == x)
            def _near():
                land[xx, rows] = both

    for away in (6, -6):
        pass_on(1, away)

    def onward_dy(i, _):
        onward(0, i)
        return _

    lax.fori_loop(0, pairs, onward_dy, 0)

    def gates_in(i, _):
        slot = (y + i) % n
        gates_copy(slot, slot).wait_recv()
        return _

    lax.fori_loop(1, n, gates_in, 0)
    f_row = lax.broadcasted_iota(I32, (half, half), 0)
    f_col = lax.broadcasted_iota(I32, (half, half), 1)
    same = f_row // pad == f_col // pad
    upto = bits(same & (f_row <= f_col))
    block = bits(same)
    earlier = bits(
        lax.broadcasted_iota(I32, (n_grp, n_grp), 1) < lax.broadcasted_iota(I32, (n_grp, n_grp), 0)
    )
    lane_of = lax.broadcasted_iota(I32, (lanes, n_grp), 0)
    src_of = lax.broadcasted_iota(I32, (lanes, n_grp), 1) * send
    from_src = bits((lane_of >= src_of) & (lane_of < src_of + send))
    lane_f = lax.broadcasted_iota(I32, (lanes, half), 0)
    col_f = lax.broadcasted_iota(I32, (lanes, half), 1)
    slot_of = (col_f % pad) == (lane_f % send)
    rank_cols = jnp.zeros((lanes, wide), F32)
    gate_cols = jnp.zeros((lanes, wide), F32)
    for ab in range(2):
        marks = y_marks[ab * per].astype(F32)
        for m in range(1, per):
            marks = marks + y_marks[ab * per + m].astype(F32)
        picked = marks != 0.0
        count = bits(picked)
        within = dot(count, upto)
        before = dot(earlier, dot(count, block).astype(BF16))
        rank = within + before - 1.0
        rank = jnp.where(picked & (rank < room), rank, 2.0 * room).astype(BF16)
        fold_row = lax.broadcasted_iota(I32, (half, wide), 0)
        fold_col = lax.broadcasted_iota(I32, (half, wide), 1)
        fold = bits(fold_row // pad + ab * per == fold_col)
        ranks = jnp.where(slot_of, dot(from_src, rank), 0.0).astype(BF16)
        gates = jnp.where(slot_of, dot(from_src, marks.astype(BF16)), 0.0).astype(BF16)
        rank_cols = rank_cols + dot(ranks, fold)
        gate_cols = gate_cols + dot(gates, fold)
    rank_ref[...] = rank_cols.astype(BF16)
    gate_cols = gate_cols.astype(BF16)
    row_ref[...] = rank_cols.T[:8]
    slot_iota = lax.broadcasted_iota(I32, (room, lanes), 0).astype(F32).astype(BF16)

    def picks(m, _):
        row = row_ref[pl.ds(m, 1), :].astype(BF16)
        pick_ref[m] = jnp.where(row == slot_iota, jnp.ones((), BF16), jnp.zeros((), BF16))
        return _

    lax.fori_loop(0, n, picks, 0)
    def fan_copy(k, m, slot):
        src, dst = ((fan_dy, full_dy), (fan_x, full_x))[k]
        return rdma(
            src.at[m], dst.at[slot, :, my_cols], fan_ss.at[m, k], fan_rs.at[slot, k], peer(m)
        )

    def twin_copy(k, slot):
        buf = (full_dy, full_x)[k]
        return rdma(
            buf.at[slot, :, my_cols], buf.at[slot, :, my_cols],
            twin_ss.at[slot, k], twin_rs.at[slot, k], twin,
        )

    def twin_arrival(k, slot):
        buf = (full_dy, full_x)[k]
        return rdma(
            buf.at[slot, :, twin_cols], buf.at[slot, :, twin_cols],
            twin_ss.at[slot, k], twin_rs.at[slot, k], twin,
        )

    def landed(k):
        land = (l_dy, l_x)[k]

        def wait(i, _):
            for dx in range(1, NX):
                xx = (x + dx) % NX
                x_copy(k, xx, xx, i).wait_recv()
            return _

        lax.fori_loop(0, pairs, wait, 0)
        return land[...].reshape(lanes, wide)

    def spread(k):
        src, dst, rows = ((fan_dy, full_dy), (fan_x, full_x))[k] + (landed(k),)

        def one(i, _):
            m = (y + ring_offset(i, n)) % n
            out = dot(pick_ref[m], rows).astype(BF16)

            @pl.when(i < n - 1)
            def _far():
                src[m] = out
                fan_copy(k, m, y).start()

            @pl.when(i == n - 1)
            def _near():
                dst[y, :, my_cols] = out
                twin_copy(k, y).start()

            return _

        lax.fori_loop(0, n, one, 0)

    def source(i):
        return (y + n - ring_offset(i, n)) % n

    def hand_over(k, i):
        slot = source(i)
        fan_copy(k, slot, slot).wait_recv()
        twin_copy(k, slot).start()

    def columns(slot):
        return pl.ds(pl.multiple_of(slot * 2 * wide, 2 * wide), 2 * wide)

    spread(0)
    gate_slots = dot(pick_ref[y], gate_cols)
    my_lane = lax.broadcasted_iota(I32, (room, wide), 1) == y
    gate_col = jnp.sum(jnp.where(my_lane, gate_slots, 0.0), axis=1, keepdims=True)
    acc_g[...] = jnp.zeros_like(acc_g)
    acc_u[...] = jnp.zeros_like(acc_u)
    acc_b[...] = jnp.zeros_like(acc_b)

    def onward_x(i, _):
        onward(1, i)
        return _

    lax.fori_loop(0, pairs, onward_x, 0)
    spread(1)
    loads[2].wait()

    def hand_dy(i, _):
        hand_over(0, i)
        return _

    lax.fori_loop(0, n - 1, hand_dy, 0)

    def back_rows(slot, _):
        twin_arrival(0, slot).wait_recv()
        acc_b[...] += lax.dot_general(
            full_dy[slot], wd_ref[:, columns(slot)], NT, preferred_element_type=F32
        )
        return _

    lax.fori_loop(0, n, back_rows, 0)
    loads[0].wait()
    loads[1].wait()

    def multiply(slot):
        twin_arrival(1, slot).wait_recv()
        rows = columns(slot)
        xs = full_x[slot]
        acc_g[...] += dot(xs, wg_ref[rows, :])
        acc_u[...] += dot(xs, wu_ref[rows, :])

    def gather(i, _):
        hand_over(1, i)
        multiply(jnp.where(i == 0, y, source(jnp.maximum(i - 1, 0))))
        return _

    lax.fori_loop(0, n - 1, gather, 0)
    multiply(source(n - 2))

    g = acc_g[...]
    u = acc_u[...]
    b = acc_b[...]
    s = 1.0 / (1.0 + jnp.exp(-g))
    a = g * s
    q = gate_col * b
    dg_ref[...] = (q * u * (s * (1.0 + g * (1.0 - s)))).astype(BF16)
    du_ref[...] = (q * a).astype(BF16)
    gate_ref[...] = a * u * b

    def give_copy(t):
        return rdma(give.at[t], got.at[t], give_ss.at[t], give_rs.at[t], twin)

    def ret_copy(t, slot):
        return rdma(pair.at[t], back.at[slot], ret_ss.at[t], ret_rs.at[slot], peer(t))

    def target(i):
        return (y + ring_offset(i, n)) % n

    def add_pair(i):
        t = target(i)
        give_copy(t).wait_recv()
        total = (keep[t] + got[t].astype(F32)).astype(BF16)

        @pl.when(i < n - 1)
        def _far():
            pair[t] = total
            ret_copy(t, y).start()

        @pl.when(i == n - 1)
        def _near():
            back[y] = total

    def produce(i, _):
        t = target(i)
        rows = pl.ds(pl.multiple_of(t * 2 * wide, 2 * wide), 2 * wide)
        part = lax.dot_general(dg_ref[...], wg_ref[rows, :], NT, preferred_element_type=F32)
        part = part + lax.dot_general(du_ref[...], wu_ref[rows, :], NT, preferred_element_type=F32)
        left, right = part[:, :wide], part[:, wide:]
        keep[t] = jnp.where(core == 0, left, right)
        give[t] = jnp.where(core == 0, right, left).astype(BF16)
        give_copy(t).start()

        @pl.when(i > 0)
        def _before():
            add_pair(jnp.maximum(i - 1, 0))

        return _

    lax.fori_loop(0, n, produce, 0)
    add_pair(n - 1)
    gate_part = gate_ref[...]
    high = gate_part.astype(BF16)
    low = (gate_part - high.astype(F32)).astype(BF16)
    ones = jnp.ones((8, gate_part.shape[1]), BF16)
    c_half = lax.dot_general(ones, high, NT, preferred_element_type=F32) + lax.dot_general(
        ones, low, NT, preferred_element_type=F32
    )
    c_own[...] = c_half.astype(BF16).astype(F32)
    rdma(c_own, c_got, cx_ss, cx_rs, twin).start()

    acc[...] = jnp.zeros_like(acc)
    lane_iota = lax.broadcasted_iota(I32, (lanes, room), 1).astype(F32)
    pick_row = lax.broadcasted_iota(I32, (wide, room), 0)

    def combine(slot):
        rank = dot(rank_ref[...], bits(pick_row == slot))
        pick = bits(rank == lane_iota)
        acc[...] += dot(pick, back[slot])

    combine(y)

    rdma(c_own, c_got, cx_ss, cx_rs, twin).wait_recv()
    c_lane = dot((c_own[...] + c_got[...]).astype(BF16), pick_ref[y])[:1, :]
    lane_to = lax.broadcasted_iota(I32, (n_grp, lanes), 1)
    src_to = lax.broadcasted_iota(I32, (n_grp, lanes), 0) * send
    c_rows = jnp.where((lane_to >= src_to) & (lane_to < src_to + send), c_lane, 0.0)
    c_spot = bits(col_f - x * part == lane_f % send)
    table = dot(c_rows.astype(BF16), c_spot)
    for xx in range(NX):
        o_c[xx] = table[xx * nz : (xx + 1) * nz]

    def home_c(to, slot):
        return rdma(o_c.at[to], m_c.at[slot], hc_ss.at[to], hc_rs.at[slot], at_x(to))

    for dx in range(1, NX):
        home_c((x + dx) % NX, x).start()

    def collect(i, _):
        slot = source(i)
        ret_copy(slot, slot).wait_recv()
        combine(slot)
        return _

    lax.fori_loop(0, n - 1, collect, 0)

    total = acc[...].astype(BF16).reshape(NX, nz * send, wide)
    def home_x(to, slot, j):
        rows = pair_rows(j)
        return rdma(
            o_x.at[to, rows], m_x.at[slot, rows], hx_ss.at[to, j], hx_rs.at[slot, j], at_x(to)
        )

    for xx in range(NX):

        @pl.when(xx != x)
        def _far():
            o_x[xx] = total[xx]

        @pl.when(xx == x)
        def _near():
            m_x[xx] = total[xx]

    def home_order(i):
        return (z // 2 + ring_offset(i, pairs)) % pairs

    def home_send(i, _):
        for dx in range(1, NX):
            home_x((x + dx) % NX, x, home_order(i)).start()
        return _

    lax.fori_loop(0, pairs, home_send, 0)

    def home_z(k, to, slot):
        src, dst = ((zo_x, h_x), (s_c, h_c))[k]
        return rdma(src.at[to], dst.at[slot], hz_ss.at[k, to], hz_rs.at[k, slot], at_z(to))

    for dx in range(1, NX):
        xx = (x + dx) % NX
        home_c(xx, xx).wait_recv()
    merged = o_c[x]
    for dx in range(1, NX):
        merged = merged + m_c[(x + dx) % NX]
    for zz in range(nz):
        s_c[zz] = merged[zz : zz + 1]

    def off_c(i, _):
        home_z(1, (z + ring_offset(i, nz)) % nz, z).start()
        return _

    lax.fori_loop(0, nz - 1, off_c, 0)

    def off(i, _):
        j = home_order(i)
        rows = pair_rows(j)
        for dx in range(1, NX):
            xx = (x + dx) % NX
            home_x(xx, xx, j).wait_recv()
        parts = [m_x[xx, rows].astype(F32) for xx in range(NX)]
        for zz in range(2):
            to = 2 * j + zz
            zo_x[to] = jnp.concatenate(
                [part[zz * send : (zz + 1) * send] for part in parts], axis=0
            ).astype(BF16)

            @pl.when(to != z)
            def _far():
                home_z(0, to, z).start()

        return _

    lax.fori_loop(0, pairs, off, 0)
    h_x[z] = zo_x[z]
    h_c[z] = s_c[z]

    def home_in(k):
        def one(i, _):
            slot = (z + i) % nz
            home_z(k, slot, slot).wait_recv()
            return _

        lax.fori_loop(1, nz, one, 0)

    home_in(1)
    for zz in range(nz):
        c_all[y, zz : zz + 1, :] = h_c[zz]

    def c_copy(t, slot):
        return rdma(c_all.at[y], c_all.at[slot], cr_ss.at[t], cr_rs.at[slot], peer(t))

    def c_send(i, _):
        c_copy(target(i), y).start()
        return _

    lax.fori_loop(0, n - 1, c_send, 0)
    home_in(0)

    def c_in(i, _):
        c_copy(source(i), source(i)).wait_recv()
        return _

    lax.fori_loop(0, n - 1, c_in, 0)
    out_x[...] = h_x[...]
    out_c[...] = c_all[...]

    def drain_z(i, _):
        to = (z + i) % nz
        meta_copy(to, z).wait_send()
        home_z(0, to, z).wait_send()
        home_z(1, to, z).wait_send()
        return _

    lax.fori_loop(1, nz, drain_z, 0)
    for dx in range(1, NX):
        to = (x + dx) % NX
        marks_copy(to, x).wait_send()
        home_c(to, x).wait_send()

        def drain_x(j, _, to=to):
            x_copy(0, to, x, j).wait_send()
            x_copy(1, to, x, j).wait_send()
            home_x(to, x, j).wait_send()
            return _

        lax.fori_loop(0, pairs, drain_x, 0)

    for k in range(2):
        for away in (0, 3, -3, 6, -6):
            for idx, hop in passes(k, away):
                ag_copy(k, z, idx, hop).wait_send()

    def drain_y(i, _):
        t = target(i)
        gates_copy(t, y).wait_send()
        fan_copy(0, t, y).wait_send()
        fan_copy(1, t, y).wait_send()
        ret_copy(t, y).wait_send()
        c_copy(t, y).wait_send()
        return _

    lax.fori_loop(0, n - 1, drain_y, 0)

    def drain_twin(i, _):
        twin_copy(0, i).wait_send()
        twin_copy(1, i).wait_send()
        give_copy(i).wait_send()
        return _

    lax.fori_loop(0, n, drain_twin, 0)
    rdma(c_own, c_got, cx_ss, cx_rs, twin).wait_send()


def routed(x, dy, marks, wg, wu, wd, n, room, send):
    nz = marks.shape[0]
    tok, wide = x.shape
    chunk = NX * send
    lanes = nz * chunk
    tokens = (nz, tok, wide)
    packed = (nz, chunk, wide)
    hidden = wg.shape[1]
    pairs = nz // 2
    dma = pltpu.SemaphoreType.DMA
    block = (n, room, wide)
    by_x = (NX, lanes // NX, wide)
    vmem = pl.BlockSpec(memory_space=pltpu.VMEM)
    hbm = pl.BlockSpec(memory_space=pl.ANY)
    half = META // 2
    return pl.pallas_call(
        kernel,
        out_shape=(
            jax.ShapeDtypeStruct(packed, BF16),
            jax.ShapeDtypeStruct((n, nz, half), F32),
        ),
        in_specs=[vmem] * 3 + [hbm] * 3,
        out_specs=(vmem, vmem),
        scratch_shapes=[
            pltpu.VMEM(wg.shape, BF16),
            pltpu.VMEM(wu.shape, BF16),
            pltpu.VMEM(wd.shape, BF16),
            pltpu.VMEM(tokens, BF16),
            pltpu.VMEM(tokens, BF16),
            pltpu.VMEM((nz * 8, half), F32),
            pltpu.VMEM((nz, chunk, half), BF16),
            pltpu.VMEM(by_x, BF16),
            pltpu.VMEM(by_x, BF16),
            pltpu.VMEM(by_x, BF16),
            pltpu.VMEM(by_x, BF16),
            pltpu.VMEM((nz, half), F32),
            pltpu.VMEM((NX * nz, half), F32),
            pltpu.VMEM((n, NX * nz, half), BF16),
            pltpu.VMEM((n, room, lanes), BF16),
            pltpu.VMEM((lanes, wide), BF16),
            pltpu.VMEM((8, lanes), F32),
            pltpu.VMEM(block, BF16),
            pltpu.VMEM(block, BF16),
            pltpu.VMEM((n, room, 2 * wide), BF16),
            pltpu.VMEM((n, room, 2 * wide), BF16),
            pltpu.VMEM((room, hidden), F32),
            pltpu.VMEM((room, hidden), F32),
            pltpu.VMEM((room, hidden), F32),
            pltpu.VMEM((room, hidden), BF16),
            pltpu.VMEM((room, hidden), BF16),
            pltpu.VMEM(block, F32),
            pltpu.VMEM(block, BF16),
            pltpu.VMEM(block, BF16),
            pltpu.VMEM(block, BF16),
            pltpu.VMEM(block, BF16),
            pltpu.VMEM((room, hidden), F32),
            pltpu.VMEM((8, room), F32),
            pltpu.VMEM((8, room), F32),
            pltpu.VMEM((n, nz, half), F32),
            pltpu.VMEM((lanes, wide), F32),
            pltpu.VMEM(by_x, BF16),
            pltpu.VMEM(by_x, BF16),
            pltpu.VMEM(packed, BF16),
            pltpu.VMEM((NX, nz, half), F32),
            pltpu.VMEM((NX, nz, half), F32),
            pltpu.VMEM((nz, 1, half), F32),
            pltpu.VMEM((nz, 1, half), F32),
            pltpu.VMEM(packed, BF16),
            dma((3,)),
            dma((nz,)),
            dma((nz,)),
            dma((2, 16)),
            dma((2, nz)),
            dma((2, NX, pairs)),
            dma((2, NX, pairs)),
            dma((NX,)),
            dma((NX,)),
            dma((n,)),
            dma((n,)),
            dma((n, 2)),
            dma((n, 2)),
            dma((n, 2)),
            dma((n, 2)),
            dma((n,)),
            dma((n,)),
            dma((n,)),
            dma((n,)),
            dma,
            dma,
            dma((n,)),
            dma((n,)),
            dma((NX, pairs)),
            dma((NX, pairs)),
            dma((NX,)),
            dma((NX,)),
            dma((2, nz)),
            dma((2, nz)),
        ],
        compiler_params=pltpu.CompilerParams(
            collective_id=0, has_side_effects=True, vmem_limit_bytes=48 << 20
        ),
        cost_estimate=pl.CostEstimate(
            flops=10 * room * hidden * n * 2 * wide, bytes_accessed=8 << 20, transcendentals=0
        ),
    )(x, dy, marks, wg, wu, wd)


def shards(inputs, out_grad, expert_ids, gate_probs, group_slot, w_gate, w_up, w_down):
    n_grp = lax.axis_size("grp")
    n_loc = lax.axis_size("loc")
    exp_grp = n_loc // 2
    tok, wide = inputs.shape
    room = 2 * tok
    send = max(1, 3 * tok // 16)
    lanes = n_grp * send
    nz = n_grp // NX
    part = META // 2 // NX

    group = expert_ids // exp_grp
    member = expert_ids % exp_grp
    sent = group_slot < send
    order = group % nz * NX + group // nz
    lane = jnp.where(sent, order * send + group_slot, lanes)
    place = jnp.any(
        lane.T[None] == jnp.arange(lanes, dtype=I32)[:, None, None], axis=1
    ).astype(BF16)
    field = jnp.where(sent, member * part + group_slot, exp_grp * part).reshape(-1)
    of_group = (order.reshape(-1)[None, :] == jnp.arange(n_grp, dtype=I32)[:, None]).astype(BF16)
    of_field = field[:, None] == jnp.arange(exp_grp * part, dtype=I32)[None, :]
    here = sent & (member == lax.axis_index("loc") // 2)
    own = jnp.where(here, group_slot, META).reshape(-1)[:, None]
    own = own == jnp.arange(part, dtype=I32)[None, :]
    marks = dot(
        of_group, jnp.where(own, gate_probs.reshape(-1)[:, None], jnp.zeros((), BF16))
    ).reshape(nz, 1, META // 2)
    spots = jnp.where(
        (order.T[None] == jnp.arange(n_grp, dtype=I32)[:, None, None]) & sent.T[None],
        group_slot.T[None],
        META,
    )
    spots = jnp.min(spots, axis=1).astype(F32).reshape(nz, NX, tok)
    spots = jnp.pad(spots, ((0, 0), (0, 0), (0, META // 2 - tok)), constant_values=META)
    meta = jnp.concatenate([spots, marks, jnp.zeros((nz, 7 - NX, META // 2), F32)], axis=1)
    home_x, home_c = routed(
        inputs,
        out_grad,
        meta,
        w_gate[0],
        w_up[0],
        w_down[0],
        exp_grp,
        room,
        send,
    )
    in_grad = lax.dot_general(
        place,
        home_x.reshape(lanes, wide),
        (((0,), (0,)), ((), ())),
        preferred_element_type=F32,
    ).astype(BF16)
    table = home_c.reshape(exp_grp, nz, NX, part).transpose(1, 2, 0, 3).reshape(n_grp, -1)
    picks = lax.dot_general(
        of_group, table.astype(BF16), (((0,), (0,)), ((), ())), preferred_element_type=F32
    )
    gate_grad = jnp.sum(jnp.where(of_field, picks, 0.0), axis=1).astype(BF16)
    return in_grad, gate_grad.reshape(expert_ids.shape)


def solution(mesh):
    return jax.shard_map(
        shards,
        mesh=mesh,
        in_specs=(
            P("grp", "loc"),
            P("grp", "loc"),
            P("grp", None),
            P("grp", None),
            P("grp", None),
            P(("grp", "loc"), None, None),
            P(("grp", "loc"), None, None),
            P(("grp", "loc"), None, None),
        ),
        out_specs=(P("grp", "loc"), P("grp", None)),
        check_vma=False,
    )
```

```python
import jax
import jax.numpy as jnp
from jax import lax
from jax.experimental import pallas as pl
from jax.experimental.pallas import tpu as pltpu
from jax.sharding import PartitionSpec as P

MESH = pl.DeviceIdType.MESH
F32 = jnp.float32
BF16 = jnp.bfloat16
I32 = jnp.int32
NX = 4
META = 256
NT = (((1,), (1,)), ((), ()))


def dot(a, b):
    return jnp.dot(a, b, preferred_element_type=F32)


def bits(mask):
    return mask.astype(F32).astype(BF16)


def ring_offset(i, n):
    half = (i + 1) // 2
    return n // 2 + jnp.where(i % 2 == 0, half, -half)


def near_offset(i, n):
    half = (i + 1) // 2
    return jnp.where(i % 2 == 0, n - half, half) % n


def kernel(
    x_ref, dy_ref, marks_ref, wg_hbm, wu_hbm, wd_hbm,
    out_x, out_c,
    wg_ref, wu_ref, wd_ref,
    raw_dy, raw_x, z_marks, place_ref, x_dy, x_x, l_dy, l_x, x_marks, l_marks, y_marks,
    pick_ref, rank_ref, row_ref, home_ref,
    fan_x, fan_dy, full_x, full_dy, acc_g, acc_u, acc_b, dg_ref, du_ref,
    keep, give, got, pair, back, gate_ref, c_own, c_got, c_all, acc,
    o_x, m_x, h_x, o_c, m_c, s_c, h_c, zo_x,
    w_sem, z_ss, z_rs, ag_ss, ag_rs, x_ss, x_rs, xm_ss, xm_rs, ym_ss, ym_rs,
    fan_ss, fan_rs, twin_ss, twin_rs, give_ss, give_rs, ret_ss, ret_rs,
    cx_ss, cx_rs, cr_ss, cr_rs, hx_ss, hx_rs, hc_ss, hc_rs, hz_ss, hz_rs,
):
    n = full_x.shape[0]
    room, wide = fan_x.shape[1:]
    nz, chunk = zo_x.shape[:2]
    tok = x_ref.shape[0]
    send = chunk // NX
    two = 2 * send
    pairs = nz // 2
    lanes = nz * chunk
    n_grp = NX * nz
    half = META // 2
    grp = lax.axis_index("grp")
    loc = lax.axis_index("loc")
    x, z = grp // nz, grp % nz
    y, core = loc // 2, loc % 2
    twin = (grp, 2 * y + 1 - core)

    def rdma(src, dst, ss, rs, to):
        return pltpu.make_async_remote_copy(
            src_ref=src, dst_ref=dst, send_sem=ss, recv_sem=rs, device_id=to, device_id_type=MESH
        )

    def at_z(zz):
        return (x * nz + zz, loc)

    def at_x(xx):
        return (xx * nz + z, loc)

    def peer(yy):
        return (grp, 2 * yy + core)

    loads = [
        pltpu.make_async_copy(src, dst, w_sem.at[i])
        for i, (src, dst) in enumerate(((wg_hbm, wg_ref), (wu_hbm, wu_ref), (wd_hbm, wd_ref)))
    ]
    for load in loads:
        load.start()

    barrier = pltpu.get_barrier_semaphore()

    def greet(to):
        pl.semaphore_signal(barrier, inc=1, device_id=to, device_id_type=MESH)

    def greet_z(i, _):
        greet(at_z((z + i) % nz))
        return _

    def greet_y(i, _):
        greet(peer((y + i) % n))
        return _

    lax.fori_loop(1, nz, greet_z, 0)
    for dx in range(1, NX):
        greet(at_x((x + dx) % NX))
    lax.fori_loop(1, n, greet_y, 0)
    greet(twin)
    pl.semaphore_wait(barrier, nz - 1 + NX - 1 + n - 1 + 1)

    def eight(slot):
        return pl.ds(pl.multiple_of(slot * 8, 8), 8)

    def ag_copy(k, block, idx, hop):
        raw = (raw_dy, raw_x)[k]
        return rdma(
            raw.at[block], raw.at[block], ag_ss.at[k, idx], ag_rs.at[k, block],
            at_z((z + hop + nz) % nz),
        )

    def passes(k, away):
        if away == 0:
            return ((0, 3), (1, -3), (2, 1), (3, -1))
        sign = 1 if away > 0 else -1
        base = {3: 4, -3: 7, 6: 10, -6: 13}[away]
        hops = ((base, 3 * sign), (base + 1, sign), (base + 2, -sign))
        if abs(away) == 3:
            return hops
        last = ((base + 2, 2 * sign),) if k == (0 if sign > 0 else 1) else ()
        return ((base, sign), (base + 1, -sign)) + last

    def arrived(k, block):
        ag_copy(k, block, 0, 1).wait_recv()

    def pass_on(k, away):
        block = (z - away + nz) % nz
        if away != 0:
            arrived(k, block)
        for idx, hop in passes(k, away):
            ag_copy(k, block, idx, hop).start()

    def meta_copy(to, slot):
        return rdma(
            marks_ref.at[to], z_marks.at[eight(slot)], z_ss.at[to], z_rs.at[slot], at_z(to)
        )

    raw_dy[z] = dy_ref[...]
    pass_on(0, 0)

    def meta_send(i, _):
        meta_copy((z + ring_offset(i, nz)) % nz, z).start()
        return _

    lax.fori_loop(0, nz - 1, meta_send, 0)
    z_marks[eight(z)] = marks_ref[z]
    raw_x[z] = x_ref[...]
    for away in (3, -3):
        pass_on(0, away)
    pass_on(1, 0)

    def meta_in(i, _):
        meta_copy((z + i) % nz, (z + i) % nz).wait_recv()
        return _

    lax.fori_loop(1, nz, meta_in, 0)

    def all_z(slot):
        return pl.ds(pl.multiple_of(slot * nz, 8), nz)

    def marks_copy(to, slot):
        return rdma(x_marks, l_marks.at[all_z(slot)], xm_ss.at[to], xm_rs.at[slot], at_x(to))

    x_marks[...] = z_marks[pl.ds(NX, nz, 8), :]
    l_marks[all_z(x)] = x_marks[...]
    for dx in range(1, NX):
        marks_copy((x + dx) % NX, x).start()
    for k, away in ((0, 6), (0, -6), (1, 3), (1, -3)):
        pass_on(k, away)
    slot_rows = lax.broadcasted_iota(I32, (send, half), 0).astype(F32)

    def chosen_rows(rows):
        return jnp.concatenate([(row == slot_rows).astype(F32) for row in rows], axis=0)

    def place(i, _):
        rows = [z_marks[pl.ds(i * 8 + xx, 1), :] for xx in range(NX)]
        place_ref[i] = chosen_rows(rows).astype(BF16)
        return _

    lax.fori_loop(0, nz, place, 0)
    for dx in range(1, NX):
        marks_copy((x + dx) % NX, (x + dx) % NX).wait_recv()
    pad = META // n
    per = half // pad
    part = half // NX
    take_row = lax.broadcasted_iota(I32, (half, half), 0)
    take_col = lax.broadcasted_iota(I32, (half, half), 1)
    inside = (take_row >= x * part) & (take_row < x * part + part)
    take = bits(inside & (take_row - x * part == take_col - (y % per) * pad))
    y_marks[y] = dot(l_marks[...].astype(BF16), take).astype(BF16)

    def gates_copy(to, slot):
        return rdma(y_marks.at[y], y_marks.at[slot], ym_ss.at[to], ym_rs.at[slot], peer(to))

    def gates_send(i, _):
        gates_copy((y + ring_offset(i, n)) % n, y).start()
        return _

    lax.fori_loop(0, n - 1, gates_send, 0)

    def pair_rows(j):
        return pl.ds(pl.multiple_of(j * two, 16 if two % 16 == 0 else 1), two)

    def x_copy(k, to, slot, j):
        src, dst = ((x_dy, l_dy), (x_x, l_x))[k]
        rows = pair_rows(j)
        return rdma(
            src.at[to, rows], dst.at[slot, rows], x_ss.at[k, to, j], x_rs.at[k, slot, j], at_x(to)
        )

    def onward(k, i):
        raw, out, land = ((raw_dy, x_dy, l_dy), (raw_x, x_x, l_x))[k]
        j = (z // 2 + near_offset(i, pairs)) % pairs
        chosen = []
        for zz in range(2):
            slot = 2 * j + zz
            away = (z - slot + nz) % nz
            passed = (away == 0) | (away == 3) | (away == 6) | (away == nz - 3) | (away == nz - 6)

            @pl.when(jnp.logical_not(passed))
            def _arrival():
                arrived(k, slot)

            chosen.append(dot(place_ref[slot][:, :tok], raw[slot]))
        even, odd = chosen
        rows = pair_rows(j)
        for xx in range(NX):
            mine = slice(xx * send, (xx + 1) * send)
            both = jnp.concatenate([even[mine], odd[mine]], axis=0).astype(BF16)

            @pl.when(xx != x)
            def _far():
                out[xx, rows] = both
                x_copy(k, xx, x, j).start()

            @pl.when(xx == x)
            def _near():
                land[xx, rows] = both

    for away in (6, -6):
        pass_on(1, away)

    def onward_dy(i, _):
        onward(0, i)
        return _

    lax.fori_loop(0, pairs, onward_dy, 0)

    def gates_in(i, _):
        slot = (y + i) % n
        gates_copy(slot, slot).wait_recv()
        return _

    lax.fori_loop(1, n, gates_in, 0)
    f_row = lax.broadcasted_iota(I32, (half, half), 0)
    f_col = lax.broadcasted_iota(I32, (half, half), 1)
    same = f_row // pad == f_col // pad
    upto = bits(same & (f_row <= f_col))
    block = bits(same)
    earlier = bits(
        lax.broadcasted_iota(I32, (n_grp, n_grp), 1) < lax.broadcasted_iota(I32, (n_grp, n_grp), 0)
    )
    lane_of = lax.broadcasted_iota(I32, (lanes, n_grp), 0)
    src_of = lax.broadcasted_iota(I32, (lanes, n_grp), 1) * send
    from_src = bits((lane_of >= src_of) & (lane_of < src_of + send))
    lane_f = lax.broadcasted_iota(I32, (lanes, half), 0)
    col_f = lax.broadcasted_iota(I32, (lanes, half), 1)
    slot_of = (col_f % pad) == (lane_f % send)
    rank_cols = jnp.zeros((lanes, wide), F32)
    gate_cols = jnp.zeros((lanes, wide), F32)
    for ab in range(2):
        marks = y_marks[ab * per].astype(F32)
        for m in range(1, per):
            marks = marks + y_marks[ab * per + m].astype(F32)
        picked = marks != 0.0
        count = bits(picked)
        within = dot(count, upto)
        before = dot(earlier, dot(count, block).astype(BF16))
        rank = within + before - 1.0
        rank = jnp.where(picked & (rank < room), rank, 2.0 * room).astype(BF16)
        fold_row = lax.broadcasted_iota(I32, (half, wide), 0)
        fold_col = lax.broadcasted_iota(I32, (half, wide), 1)
        fold = bits(fold_row // pad + ab * per == fold_col)
        ranks = jnp.where(slot_of, dot(from_src, rank), 0.0).astype(BF16)
        gates = jnp.where(slot_of, dot(from_src, marks.astype(BF16)), 0.0).astype(BF16)
        rank_cols = rank_cols + dot(ranks, fold)
        gate_cols = gate_cols + dot(gates, fold)
    rank_ref[...] = rank_cols.astype(BF16)
    gate_cols = gate_cols.astype(BF16)
    row_ref[...] = rank_cols.T[:8]
    slot_iota = lax.broadcasted_iota(I32, (room, lanes), 0).astype(F32).astype(BF16)

    def picks(m, _):
        row = row_ref[pl.ds(m, 1), :].astype(BF16)
        pick_ref[m] = jnp.where(row == slot_iota, jnp.ones((), BF16), jnp.zeros((), BF16))
        return _

    lax.fori_loop(0, n, picks, 0)
    def fan_copy(k, m, slot):
        src, dst = ((fan_dy, full_dy), (fan_x, full_x))[k]
        return rdma(
            src.at[m], dst.at[slot, core], fan_ss.at[m, k], fan_rs.at[slot, k], peer(m)
        )

    def twin_copy(k, slot):
        buf = (full_dy, full_x)[k]
        return rdma(
            buf.at[slot, core], buf.at[slot, core],
            twin_ss.at[slot, k], twin_rs.at[slot, k], twin,
        )

    def twin_arrival(k, slot):
        buf = (full_dy, full_x)[k]
        return rdma(
            buf.at[slot, 1 - core], buf.at[slot, 1 - core],
            twin_ss.at[slot, k], twin_rs.at[slot, k], twin,
        )

    def landed(k):
        land = (l_dy, l_x)[k]

        def wait(i, _):
            for dx in range(1, NX):
                xx = (x + dx) % NX
                x_copy(k, xx, xx, i).wait_recv()
            return _

        lax.fori_loop(0, pairs, wait, 0)
        return land[...].reshape(lanes, wide)

    def spread(k):
        src, dst, rows = ((fan_dy, full_dy), (fan_x, full_x))[k] + (landed(k),)

        def one(i, _):
            m = (y + ring_offset(i, n)) % n
            out = dot(pick_ref[m], rows).astype(BF16)

            @pl.when(i < n - 1)
            def _far():
                src[m] = out
                fan_copy(k, m, y).start()

            @pl.when(i == n - 1)
            def _near():
                dst[y, core] = out
                twin_copy(k, y).start()

            return _

        lax.fori_loop(0, n, one, 0)

    def source(i):
        return (y + n - ring_offset(i, n)) % n

    def hand_over(k, i):
        slot = source(i)
        fan_copy(k, slot, slot).wait_recv()
        twin_copy(k, slot).start()

    def columns(slot):
        return pl.ds(pl.multiple_of(slot * 2 * wide, 2 * wide), 2 * wide)

    spread(0)
    gate_slots = dot(pick_ref[y], gate_cols)
    my_lane = lax.broadcasted_iota(I32, (room, wide), 1) == y
    gate_col = jnp.sum(jnp.where(my_lane, gate_slots, 0.0), axis=1, keepdims=True)
    acc_g[...] = jnp.zeros_like(acc_g)
    acc_u[...] = jnp.zeros_like(acc_u)
    acc_b[...] = jnp.zeros_like(acc_b)

    def onward_x(i, _):
        onward(1, i)
        return _

    lax.fori_loop(0, pairs, onward_x, 0)
    spread(1)
    loads[2].wait()

    def hand_dy(i, _):
        hand_over(0, i)
        return _

    lax.fori_loop(0, n - 1, hand_dy, 0)

    def back_rows(slot, _):
        twin_arrival(0, slot).wait_recv()
        acc_b[...] += lax.dot_general(
            jnp.concatenate([full_dy[slot, 0], full_dy[slot, 1]], axis=1),
            wd_ref[:, columns(slot)], NT, preferred_element_type=F32
        )
        return _

    lax.fori_loop(0, n, back_rows, 0)
    loads[0].wait()
    loads[1].wait()

    def multiply(slot):
        twin_arrival(1, slot).wait_recv()
        rows = columns(slot)
        xs = jnp.concatenate([full_x[slot, 0], full_x[slot, 1]], axis=1)
        acc_g[...] += dot(xs, wg_ref[rows, :])
        acc_u[...] += dot(xs, wu_ref[rows, :])

    def gather(i, _):
        hand_over(1, i)
        multiply(jnp.where(i == 0, y, source(jnp.maximum(i - 1, 0))))
        return _

    lax.fori_loop(0, n - 1, gather, 0)
    multiply(source(n - 2))

    g = acc_g[...]
    u = acc_u[...]
    b = acc_b[...]
    s = 1.0 / (1.0 + jnp.exp(-g))
    a = g * s
    q = gate_col * b
    dg_ref[...] = (q * u * (s * (1.0 + g * (1.0 - s)))).astype(BF16)
    du_ref[...] = (q * a).astype(BF16)
    gate_ref[...] = a * u * b

    def give_copy(t):
        return rdma(give.at[t], got.at[t], give_ss.at[t], give_rs.at[t], twin)

    def ret_copy(t, slot):
        return rdma(pair.at[t], back.at[slot], ret_ss.at[t], ret_rs.at[slot], peer(t))

    def target(i):
        return (y + ring_offset(i, n)) % n

    def add_pair(i):
        t = target(i)
        give_copy(t).wait_recv()
        total = (keep[t] + got[t].astype(F32)).astype(BF16)

        @pl.when(i < n - 1)
        def _far():
            pair[t] = total
            ret_copy(t, y).start()

        @pl.when(i == n - 1)
        def _near():
            back[y] = total

    def produce(i, _):
        t = target(i)
        rows = pl.ds(pl.multiple_of(t * 2 * wide, 2 * wide), 2 * wide)
        part = lax.dot_general(dg_ref[...], wg_ref[rows, :], NT, preferred_element_type=F32)
        part = part + lax.dot_general(du_ref[...], wu_ref[rows, :], NT, preferred_element_type=F32)
        left, right = part[:, :wide], part[:, wide:]
        keep[t] = jnp.where(core == 0, left, right)
        give[t] = jnp.where(core == 0, right, left).astype(BF16)
        give_copy(t).start()

        @pl.when(i > 0)
        def _before():
            add_pair(jnp.maximum(i - 1, 0))

        return _

    lax.fori_loop(0, n, produce, 0)
    add_pair(n - 1)
    gate_part = gate_ref[...]
    high = gate_part.astype(BF16)
    low = (gate_part - high.astype(F32)).astype(BF16)
    ones = jnp.ones((8, gate_part.shape[1]), BF16)
    c_half = lax.dot_general(ones, high, NT, preferred_element_type=F32) + lax.dot_general(
        ones, low, NT, preferred_element_type=F32
    )
    c_own[...] = c_half.astype(BF16).astype(F32)
    rdma(c_own, c_got, cx_ss, cx_rs, twin).start()

    acc[...] = jnp.zeros_like(acc)
    lane_iota = lax.broadcasted_iota(I32, (lanes, room), 1).astype(F32)
    pick_row = lax.broadcasted_iota(I32, (wide, room), 0)

    def combine(slot, wait=None):
        rank = dot(rank_ref[...], bits(pick_row == slot))
        pick = bits(rank == lane_iota)
        if wait is not None:
            wait.wait_recv()
        acc[...] += dot(pick, back[slot])

    combine(y)

    for zz in range(nz):
        rows = [marks_ref[zz, xx : xx + 1, :] for xx in range(NX)]
        place_ref[zz] = chosen_rows(rows).astype(BF16)
    home_place = place_ref[...].astype(F32).reshape(lanes, half).T
    home_ref[...] = home_place[:tok].astype(BF16)

    rdma(c_own, c_got, cx_ss, cx_rs, twin).wait_recv()
    c_lane = dot((c_own[...] + c_got[...]).astype(BF16), pick_ref[y])[:1, :]
    lane_to = lax.broadcasted_iota(I32, (n_grp, lanes), 1)
    src_to = lax.broadcasted_iota(I32, (n_grp, lanes), 0) * send
    c_rows = jnp.where((lane_to >= src_to) & (lane_to < src_to + send), c_lane, 0.0)
    c_spot = bits(col_f - x * part == lane_f % send)
    table = dot(c_rows.astype(BF16), c_spot)
    for xx in range(NX):
        o_c[xx] = table[xx * nz : (xx + 1) * nz]

    def home_c(to, slot):
        return rdma(o_c.at[to], m_c.at[slot], hc_ss.at[to], hc_rs.at[slot], at_x(to))

    for dx in range(1, NX):
        home_c((x + dx) % NX, x).start()

    def collect(i, _):
        slot = source(i)
        combine(slot, ret_copy(slot, slot))
        return _

    lax.fori_loop(0, n - 1, collect, 0)

    total = acc[...].astype(BF16).reshape(NX, nz * send, wide)
    def home_x(to, slot, j):
        rows = pair_rows(j)
        return rdma(
            o_x.at[to, rows], m_x.at[slot, rows], hx_ss.at[to, j], hx_rs.at[slot, j], at_x(to)
        )

    for xx in range(NX):

        @pl.when(xx != x)
        def _far():
            o_x[xx] = total[xx]

        @pl.when(xx == x)
        def _near():
            m_x[xx] = total[xx]

    def home_order(i):
        return (z // 2 + ring_offset(i, pairs)) % pairs

    def home_send(i, _):
        for dx in range(1, NX):
            home_x((x + dx) % NX, x, home_order(i)).start()
        return _

    lax.fori_loop(0, pairs, home_send, 0)

    def home_z(k, to, slot):
        src, dst = ((zo_x, h_x), (s_c, h_c))[k]
        return rdma(src.at[to], dst.at[slot], hz_ss.at[k, to], hz_rs.at[k, slot], at_z(to))

    for dx in range(1, NX):
        xx = (x + dx) % NX
        home_c(xx, xx).wait_recv()
    merged = o_c[x]
    for dx in range(1, NX):
        merged = merged + m_c[(x + dx) % NX]
    for zz in range(nz):
        s_c[zz] = merged[zz : zz + 1]

    def off_c(i, _):
        home_z(1, (z + ring_offset(i, nz)) % nz, z).start()
        return _

    lax.fori_loop(0, nz - 1, off_c, 0)

    def off(i, _):
        j = home_order(i)
        rows = pair_rows(j)
        for dx in range(1, NX):
            xx = (x + dx) % NX
            home_x(xx, xx, j).wait_recv()
        parts = [m_x[xx, rows].astype(F32) for xx in range(NX)]
        for zz in range(2):
            to = 2 * j + zz
            zo_x[to] = jnp.concatenate(
                [part[zz * send : (zz + 1) * send] for part in parts], axis=0
            ).astype(BF16)

            @pl.when(to != z)
            def _far():
                home_z(0, to, z).start()

        return _

    lax.fori_loop(0, pairs, off, 0)
    h_x[z] = zo_x[z]
    h_c[z] = s_c[z]

    def home_in(k):
        def one(i, _):
            slot = (z + i) % nz
            home_z(k, slot, slot).wait_recv()
            return _

        lax.fori_loop(1, nz, one, 0)

    home_in(1)
    for zz in range(nz):
        c_all[y, zz : zz + 1, :] = h_c[zz]

    def c_copy(t, slot):
        return rdma(c_all.at[y], c_all.at[slot], cr_ss.at[t], cr_rs.at[slot], peer(t))

    def c_send(i, _):
        c_copy(target(i), y).start()
        return _

    lax.fori_loop(0, n - 1, c_send, 0)
    home_in(0)

    def c_in(i, _):
        c_copy(source(i), source(i)).wait_recv()
        return _

    lax.fori_loop(0, n - 1, c_in, 0)
    out_x[...] = dot(home_ref[...], h_x[...].reshape(lanes, wide)).astype(BF16)
    out_c[...] = c_all[...]

    def drain_z(i, _):
        to = (z + i) % nz
        meta_copy(to, z).wait_send()
        home_z(0, to, z).wait_send()
        home_z(1, to, z).wait_send()
        return _

    lax.fori_loop(1, nz, drain_z, 0)
    for dx in range(1, NX):
        to = (x + dx) % NX
        marks_copy(to, x).wait_send()
        home_c(to, x).wait_send()

        def drain_x(j, _, to=to):
            x_copy(0, to, x, j).wait_send()
            x_copy(1, to, x, j).wait_send()
            home_x(to, x, j).wait_send()
            return _

        lax.fori_loop(0, pairs, drain_x, 0)

    for k in range(2):
        for away in (0, 3, -3, 6, -6):
            for idx, hop in passes(k, away):
                ag_copy(k, z, idx, hop).wait_send()

    def drain_y(i, _):
        t = target(i)
        gates_copy(t, y).wait_send()
        fan_copy(0, t, y).wait_send()
        fan_copy(1, t, y).wait_send()
        ret_copy(t, y).wait_send()
        c_copy(t, y).wait_send()
        return _

    lax.fori_loop(0, n - 1, drain_y, 0)

    def drain_twin(i, _):
        twin_copy(0, i).wait_send()
        twin_copy(1, i).wait_send()
        give_copy(i).wait_send()
        return _

    lax.fori_loop(0, n, drain_twin, 0)
    rdma(c_own, c_got, cx_ss, cx_rs, twin).wait_send()


def routed(x, dy, marks, wg, wu, wd, n, room, send):
    nz = marks.shape[0]
    tok, wide = x.shape
    chunk = NX * send
    lanes = nz * chunk
    tokens = (nz, tok, wide)
    packed = (nz, chunk, wide)
    hidden = wg.shape[1]
    pairs = nz // 2
    dma = pltpu.SemaphoreType.DMA
    block = (n, room, wide)
    by_x = (NX, lanes // NX, wide)
    vmem = pl.BlockSpec(memory_space=pltpu.VMEM)
    hbm = pl.BlockSpec(memory_space=pltpu.HBM)
    half = META // 2
    return pl.pallas_call(
        kernel,
        out_shape=(
            jax.ShapeDtypeStruct((tok, wide), BF16),
            jax.ShapeDtypeStruct((n, nz, half), F32),
        ),
        in_specs=[vmem] * 3 + [hbm] * 3,
        out_specs=(vmem, vmem),
        scratch_shapes=[
            pltpu.VMEM(wg.shape, BF16),
            pltpu.VMEM(wu.shape, BF16),
            pltpu.VMEM(wd.shape, BF16),
            pltpu.VMEM(tokens, BF16),
            pltpu.VMEM(tokens, BF16),
            pltpu.VMEM((nz * 8, half), F32),
            pltpu.VMEM((nz, chunk, half), BF16),
            pltpu.VMEM(by_x, BF16),
            pltpu.VMEM(by_x, BF16),
            pltpu.VMEM(by_x, BF16),
            pltpu.VMEM(by_x, BF16),
            pltpu.VMEM((nz, half), F32),
            pltpu.VMEM((NX * nz, half), F32),
            pltpu.VMEM((n, NX * nz, half), BF16),
            pltpu.VMEM((n, room, lanes), BF16),
            pltpu.VMEM((lanes, wide), BF16),
            pltpu.VMEM((8, lanes), F32),
            pltpu.VMEM((tok, lanes), BF16),
            pltpu.VMEM(block, BF16),
            pltpu.VMEM(block, BF16),
            pltpu.VMEM((n, 2, room, wide), BF16),
            pltpu.VMEM((n, 2, room, wide), BF16),
            pltpu.VMEM((room, hidden), F32),
            pltpu.VMEM((room, hidden), F32),
            pltpu.VMEM((room, hidden), F32),
            pltpu.VMEM((room, hidden), BF16),
            pltpu.VMEM((room, hidden), BF16),
            pltpu.VMEM(block, F32),
            pltpu.VMEM(block, BF16),
            pltpu.VMEM(block, BF16),
            pltpu.VMEM(block, BF16),
            pltpu.VMEM(block, BF16),
            pltpu.VMEM((room, hidden), F32),
            pltpu.VMEM((8, room), F32),
            pltpu.VMEM((8, room), F32),
            pltpu.VMEM((n, nz, half), F32),
            pltpu.VMEM((lanes, wide), F32),
            pltpu.VMEM(by_x, BF16),
            pltpu.VMEM(by_x, BF16),
            pltpu.VMEM(packed, BF16),
            pltpu.VMEM((NX, nz, half), F32),
            pltpu.VMEM((NX, nz, half), F32),
            pltpu.VMEM((nz, 1, half), F32),
            pltpu.VMEM((nz, 1, half), F32),
            pltpu.VMEM(packed, BF16),
            dma((3,)),
            dma((nz,)),
            dma((nz,)),
            dma((2, 16)),
            dma((2, nz)),
            dma((2, NX, pairs)),
            dma((2, NX, pairs)),
            dma((NX,)),
            dma((NX,)),
            dma((n,)),
            dma((n,)),
            dma((n, 2)),
            dma((n, 2)),
            dma((n, 2)),
            dma((n, 2)),
            dma((n,)),
            dma((n,)),
            dma((n,)),
            dma((n,)),
            dma,
            dma,
            dma((n,)),
            dma((n,)),
            dma((NX, pairs)),
            dma((NX, pairs)),
            dma((NX,)),
            dma((NX,)),
            dma((2, nz)),
            dma((2, nz)),
        ],
        compiler_params=pltpu.CompilerParams(
            collective_id=0, has_side_effects=True, vmem_limit_bytes=48 << 20
        ),
        cost_estimate=pl.CostEstimate(
            flops=10 * room * hidden * n * 2 * wide, bytes_accessed=8 << 20, transcendentals=0
        ),
    )(x, dy, marks, wg, wu, wd)


def shards(inputs, out_grad, expert_ids, gate_probs, group_slot, w_gate, w_up, w_down):
    n_grp = lax.axis_size("grp")
    n_loc = lax.axis_size("loc")
    exp_grp = n_loc // 2
    tok, wide = inputs.shape
    room = 2 * tok
    send = max(1, 3 * tok // 16)
    lanes = n_grp * send
    nz = n_grp // NX
    part = META // 2 // NX

    group = expert_ids // exp_grp
    member = expert_ids % exp_grp
    sent = group_slot < send
    order = group % nz * NX + group // nz
    field = jnp.where(sent, member * part + group_slot, exp_grp * part).T.reshape(-1)
    of_group = (order.T.reshape(-1)[None, :] == jnp.arange(n_grp, dtype=I32)[:, None]).astype(BF16)
    of_field = field[:, None] == jnp.arange(exp_grp * part, dtype=I32)[None, :]
    here = sent & (member == lax.axis_index("loc") // 2)
    own = jnp.where(here, group_slot, META).T.reshape(-1)[:, None]
    own = own == jnp.arange(part, dtype=I32)[None, :]
    marks = dot(
        of_group, jnp.where(own, gate_probs.T.reshape(-1)[:, None], jnp.zeros((), BF16))
    ).reshape(nz, 1, META // 2)
    spots = jnp.where(
        (order.T[None] == jnp.arange(n_grp, dtype=I32)[:, None, None]) & sent.T[None],
        group_slot.T[None],
        META,
    )
    spots = jnp.min(spots, axis=1).astype(F32).reshape(nz, NX, tok)
    spots = jnp.pad(spots, ((0, 0), (0, 0), (0, META // 2 - tok)), constant_values=META)
    meta = jnp.concatenate([spots, marks, jnp.zeros((nz, 7 - NX, META // 2), F32)], axis=1)
    in_grad, home_c = routed(
        inputs,
        out_grad,
        meta,
        w_gate[0],
        w_up[0],
        w_down[0],
        exp_grp,
        room,
        send,
    )
    table = home_c.reshape(exp_grp, nz, NX, part).transpose(1, 2, 0, 3).reshape(n_grp, -1)
    picks = lax.dot_general(
        of_group, table.astype(BF16), (((0,), (0,)), ((), ())), preferred_element_type=F32
    )
    gate_grad = jnp.sum(jnp.where(of_field, picks, 0.0), axis=1).astype(BF16)
    return in_grad, gate_grad.reshape(expert_ids.T.shape).T


def solution(mesh):
    return jax.shard_map(
        shards,
        mesh=mesh,
        in_specs=(
            P("grp", "loc"),
            P("grp", "loc"),
            P("grp", None),
            P("grp", None),
            P("grp", None),
            P(("grp", "loc"), None, None),
            P(("grp", "loc"), None, None),
            P(("grp", "loc"), None, None),
        ),
        out_specs=(P("grp", "loc"), P("grp", None)),
        check_vma=False,
    )
```
